32 devices in a mesh: wide: 8 (over y, x, core), narrow: 4 (over z).
Axes of the slice: x: 2, y: 2, z: 4, core: 2. Of those that a mesh axis runs over, the one named last changes fastest.
Arguments:
- exposures: bfloat16 [4, 128, 3072], P(None, 'narrow', 'wide'), may hold values from -6 to 6
- basis_kernels: bfloat16 [5, 21, 21], replicated, may hold values from -0.25 to 0.25
- poly_coef: float32 [4, 5, 6], replicated, may hold values from -3 to 3
- exposure_weight: float32 [4], replicated, may hold values from 0.5 to 2
- row_start: int32 [4], replicated, may hold values from 0 to 64, as said below
- row_count: int32 [4], replicated, may hold values from 32 to 128, as said below
- filter_taps: float32 [21], replicated, may hold values from -1.5 to 1.5
Outputs:
- coadded: float32 [128, 3072], P('narrow', 'wide')
- detection: float32 [128, 3072], P('narrow', 'wide')
The draws below stay inside these ranges and needn't reach their ends.
Inputs may be any that keep to these rules, and one draw needn't show every extreme that they name: Each row_start is a multiple of 32; row_start[0] is 0 and row_start + row_count never exceeds 128. Each row_count is a multiple of 8; exposure 0 covers the whole band.
All inputs are finite; a program needn't handle non-finite values.
Results may differ from the reference program's by a relative error of at most 0.0003.
Values may be sent and summed in bfloat16 or wider, within the bound.
No kernel may reach another device: no remote copies, remote signals or barrier semaphores. Data moves between devices by JAX's collectives and lax.ppermute only.
A program may use at most 64 MiB of HBM per device.

```python
import math
import jax
import jax.numpy as jnp
from jax import lax

EXPOSURES = 4
KERNELS = 5
KSIZE = 21
TH = 32
NR = 128
NC = 3072


def coverage_table(key):
    folded = jax.random.fold_in(key, 31)
    key_start, key_count = jax.random.split(folded)
    blocks = NR // TH
    starts = TH * jax.random.randint(key_start, (EXPOSURES,), 0, blocks // 2 + 1)
    starts = starts.at[0].set(0)
    starts = starts.at[1].set(TH * (blocks // 2))
    spare_room = (NR - starts - NR // 4) // 8 + 1
    drawn_values = jax.random.randint(key_count, (EXPOSURES,), 0, 1 << 20)
    counts = NR // 4 + 8 * (drawn_values % spare_room)
    counts = counts.at[0].set(NR)
    counts = counts.at[1].set(NR // 4)
    return (starts.astype(jnp.int32), counts.astype(jnp.int32))


def draw_row_start(key, part):
    return coverage_table(key)[0]


def draw_row_count(key, part):
    return coverage_table(key)[1]


def levels(rng, shape, shards, smallest, largest):
    factor_of, own = 1.0, jax.random.fold_in(rng, 6)
    for dim, parts in shards:
        heights = jnp.exp(jax.random.uniform(jax.random.fold_in(own, dim), (parts,), jnp.float32, smallest / len(shards), largest / len(shards)))
        factor_of = factor_of * jnp.repeat(heights, shape[dim] // parts).reshape([-1 if axis == dim else 1 for axis in range(len(shape))])
    return factor_of


def scatter_about(own_key, shape, spread, limit, shards=(), kind=jnp.bfloat16):
    array = jax.random.normal(own_key, shape, jnp.float32) * spread
    if len(shards) > 0:
        array = levels(own_key, shape, shards, -0.22, 0.18) * array
    return jnp.clip(array, min=-limit, max=limit).astype(kind)


def setup_inputs(seed: int = 0) -> dict:
    splits = jax.random.split(jax.random.key(seed), 8)
    exposures = scatter_about(splits[0], (EXPOSURES, NR, NC), 1.0, 6.0, ((1, 4), (2, 8)))
    basis_kernels = scatter_about(splits[1], (KERNELS, KSIZE, KSIZE), (KSIZE * KSIZE) ** -0.5, 0.25)
    poly_coef = scatter_about(splits[2], (EXPOSURES, KERNELS, 6), 0.5, 3.0, (), jnp.float32)
    exposure_weight = jnp.clip(jnp.exp(jax.random.uniform(splits[3], (EXPOSURES,), jnp.float32, math.log(0.5), math.log(2.0))), 0.5, 2.0)
    row_start = draw_row_start(jax.random.fold_in(splits[7], 71), 0)
    row_count = draw_row_count(jax.random.fold_in(splits[7], 71), 0)
    filter_taps = scatter_about(splits[6], (KSIZE,), 0.25, 1.5, (), jnp.float32)
    return dict(exposures=exposures, basis_kernels=basis_kernels, poly_coef=poly_coef, exposure_weight=exposure_weight, row_start=row_start, row_count=row_count, filter_taps=filter_taps)


def respond(image, basis_kernels):
    padded = jnp.pad(image, 10)[None, None]
    return lax.conv_general_dilated(padded, basis_kernels[:, None], (1, 1), "VALID", dimension_numbers=("NCHW", "OIHW", "NCHW"), preferred_element_type=jnp.float32)[0]


def reference(exposures, basis_kernels, poly_coef, exposure_weight, row_start, row_count, filter_taps):
    row_index = jnp.arange(NR, dtype=jnp.int32)
    col_index = jnp.arange(NC, dtype=jnp.int32)
    y_coord = ((2 * row_index + 1).astype(jnp.float32) / NR - 1.0)[:, None]
    x_coord = ((2 * col_index + 1).astype(jnp.float32) / NC - 1.0)[None, :]
    numerator = jnp.zeros((NR, NC), jnp.float32)
    denominator = jnp.zeros((NR, 1), jnp.float32)
    for member in range(EXPOSURES):
        framed = jnp.concatenate([jnp.zeros((NR, NC), exposures.dtype), exposures[member]], 0)
        placed = lax.dynamic_slice_in_dim(framed, (NR - row_start[member]).astype(jnp.int32), NR, 0)
        inside = (row_index >= row_start[member]) & (row_index < row_start[member] + row_count[member])
        placed = jnp.where(inside[:, None], placed, jnp.zeros((), exposures.dtype))
        response = respond(placed, basis_kernels)
        matched = jnp.zeros((NR, NC), jnp.float32)
        for kernel in range(KERNELS):
            coeffs = poly_coef[member, kernel]
            spatial = coeffs[0] + coeffs[1] * x_coord + coeffs[2] * y_coord + coeffs[3] * x_coord * x_coord + coeffs[4] * x_coord * y_coord + coeffs[5] * y_coord * y_coord
            matched = matched + spatial * response[kernel]
        weighting = exposure_weight[member] * inside.astype(jnp.float32)[:, None]
        numerator = numerator + weighting * matched
        denominator = denominator + weighting
    coadded = numerator / denominator
    padded = jnp.pad(coadded, ((0, 0), (10, 10)))
    across = filter_taps[0] * padded[:, 0:NC]
    for offset in range(1, KSIZE):
        across = across + filter_taps[offset] * padded[:, offset:offset + NC]
    padded = jnp.pad(across, ((10, 10), (0, 0)))
    detection = filter_taps[0] * padded[0:NR]
    for offset in range(1, KSIZE):
        detection = detection + filter_taps[offset] * padded[offset:offset + NR]
    return coadded, detection
```

```python
import functools

import jax
import jax.numpy as jnp
from jax import lax
from jax.experimental import pallas as pl
from jax.experimental.pallas import tpu as pltpu
from jax.sharding import PartitionSpec as P

LANES = 128
VMEM_BYTES = 48 << 20


def rounded(value, unit):
    return -(-value // unit) * unit


def sizes(tile_rows, side):
    half = side // 2
    out_rows = rounded(tile_rows + 2 * half, 8)
    in_rows = rounded(tile_rows + 4 * half, 16)
    return half, out_rows, in_rows


def band_matrix_kernel(side, tile_rows, base_ref, band_ref):
    half, out_rows, in_rows = sizes(tile_rows, side)
    kernel_total, wide = base_ref.shape
    depth = band_ref.shape[1]
    lane = lax.broadcasted_iota(jnp.int32, (8, wide), 1)
    place = lax.rem(lane, in_rows)
    row = lax.broadcasted_iota(jnp.int32, (8, wide), 0)
    split = tile_rows + half
    for kernel in range(kernel_total):
        spread = jnp.broadcast_to(base_ref[kernel : kernel + 1, :], (8, wide))

        def shifted(shift, spread=spread):
            plain = pltpu.roll(spread, shift % wide, 1)
            plain = pltpu.roll(plain, 0, 1, stride=1, stride_axis=0)
            wrapped = pltpu.roll(spread, (shift + in_rows) % wide, 1)
            wrapped = pltpu.roll(wrapped, 0, 1, stride=1, stride_axis=0)
            return jnp.where(place >= tile_rows + 2 * half + 4, wrapped, plain)

        parts = []
        for first in range(0, out_rows, 8):
            if first + 8 <= split:
                block = shifted(first - half)
            elif first >= split:
                block = shifted(first - out_rows - half)
            else:
                block = jnp.where(
                    row + first < split, shifted(first - half), shifted(first - out_rows - half)
                )
            parts.append(block)
        block = jnp.concatenate(parts, axis=0)[:, :depth]
        band_ref[kernel * out_rows : (kernel + 1) * out_rows, :] = block.astype(jnp.bfloat16)


def band_matrix(basis_kernels, tile_rows):
    kernel_total, side = basis_kernels.shape[:2]
    _, out_rows, in_rows = sizes(tile_rows, side)
    depth = side * in_rows
    wide = rounded(depth, LANES)
    base = basis_kernels.astype(jnp.float32).transpose(0, 2, 1)
    base = jnp.pad(base, ((0, 0), (0, 0), (0, in_rows - side))).reshape(kernel_total, depth)
    base = jnp.pad(base, ((0, 0), (0, wide - depth)))
    return pl.pallas_call(
        functools.partial(band_matrix_kernel, side, tile_rows),
        out_shape=jax.ShapeDtypeStruct((kernel_total * out_rows, depth), jnp.bfloat16),
        compiler_params=pltpu.CompilerParams(vmem_limit_bytes=VMEM_BYTES),
        name="band_matrix",
    )(base)


def edges_kernel(rim, tile_ref, core_ref, cross_ref):
    odd = lax.rem(lax.axis_index("wide"), 2) == 1
    members, rows, columns = tile_ref.shape
    lane = lax.broadcasted_iota(jnp.int32, (rows, LANES), 1)
    leftward = jnp.zeros((rows, LANES), jnp.bfloat16)
    rightward = jnp.zeros((rows, LANES), jnp.bfloat16)
    for member in range(members):
        own = lane // 32 == member
        first = pltpu.roll(tile_ref[member, :, :LANES], 32 * member, 1)
        last = pltpu.roll(tile_ref[member, :, columns - LANES :], (32 * member + 32) % LANES, 1)
        leftward = jnp.where(own, first, leftward)
        rightward = jnp.where(own, last, rightward)

    @pl.when(odd)
    def _():
        core_ref[...] = leftward
        cross_ref[...] = rightward

    @pl.when(jnp.logical_not(odd))
    def _():
        core_ref[...] = rightward
        cross_ref[...] = leftward


def coadd_kernel(
    peers,
    wide_peers,
    side,
    coef_ref,
    weight_ref,
    start_ref,
    count_ref,
    taps_ref,
    band_ref,
    *refs,
):
    tiles, edges = refs[:peers], refs[peers : 2 * peers]
    coadd_ref, detection_ref, frame, patches, tall = refs[2 * peers :]
    members, tile_rows, tile_cols = tiles[0].shape
    half, out_rows, in_rows = sizes(tile_rows, side)
    rim = 2 * half
    total_cols = tile_cols + LANES
    kernel_total = band_ref.shape[0] // out_rows
    narrow, wide = lax.axis_index("narrow"), lax.axis_index("wide")
    odd = lax.rem(wide, 2)
    row_base = narrow * tile_rows
    band_rows, band_cols = peers * tile_rows, wide_peers * tile_cols

    edge_lane = lax.broadcasted_iota(jnp.int32, (tile_rows, LANES), 1)
    keep_after = (edge_lane < rim) & (wide < wide_peers - 1)
    keep_before = (edge_lane >= LANES - rim) & (wide > 0)
    none = jnp.zeros((tile_rows, LANES), jnp.bfloat16)
    for index in range(peers):
        slot = jnp.bitwise_xor(narrow, index)
        after = edges[index][odd]
        before = edges[index][1 - odd]
        for member in range(members):
            frame[slot, member, :, :tile_cols] = tiles[index][member]
            right = pltpu.roll(after, (LANES - 32 * member) % LANES, 1)
            left = pltpu.roll(before, (LANES + 96 - 32 * member) % LANES, 1)
            frame[slot, member, :, tile_cols:] = jnp.where(
                keep_after, right, jnp.where(keep_before, left, none)
            )

    place = lax.broadcasted_iota(jnp.int32, (out_rows, LANES), 0)
    row = row_base + jnp.where(place < tile_rows + half, place, place - out_rows)
    y_coord = (2 * row + 1).astype(jnp.float32) / band_rows - 1.0
    lane = lax.broadcasted_iota(jnp.int32, (8, total_cols), 1)
    column = wide * tile_cols + jnp.where(lane < tile_cols + LANES // 2, lane, lane - total_cols)
    x_coord = ((2 * column + 1).astype(jnp.float32) / band_cols - 1.0)[:1]
    in_band = (column >= 0) & (column < band_cols)
    weighting = []
    for member in range(members):
        inside = (row >= start_ref[member]) & (row < start_ref[member] + count_ref[member])
        weighting.append(jnp.where(inside, weight_ref[member], 0.0))
    denominator = functools.reduce(jnp.add, weighting)
    valid = (row >= 0) & (row < band_rows)
    inverse = jnp.where(valid, 1.0 / jnp.where(valid, denominator, 1.0), 0.0)

    in_place = lax.broadcasted_iota(jnp.int32, (in_rows, total_cols), 0)
    in_offset = jnp.where(in_place < tile_rows + rim + 4, in_place, in_place - in_rows)
    sums = [jnp.zeros((out_rows, total_cols), jnp.float32) for _ in range(3)]

    def over_columns(array):
        return jnp.concatenate([array] * (total_cols // LANES), axis=1)

    for member in range(members):
        slot = narrow - start_ref[member] // tile_rows
        here = jnp.clip(slot, 0, peers - 1)
        above = jnp.clip(slot - 1, 0, peers - 1)
        below = jnp.clip(slot + 1, 0, peers - 1)
        mixed = lax.broadcasted_iota(jnp.int32, (16, total_cols), 0) < 8
        window = jnp.concatenate(
            [
                frame[here, member],
                frame[below, member, :16],
                jnp.where(mixed, frame[below, member, 16:], frame[above, member, :16]),
                frame[above, member, 16:],
            ],
            axis=0,
        )
        frame_row = in_offset + (row_base - start_ref[member])
        present = (frame_row >= 0) & (frame_row < count_ref[member])
        window = jnp.where(present, window, jnp.zeros((), window.dtype))
        for tap in range(side):
            patches[member, tap * in_rows : (tap + 1) * in_rows, :] = pltpu.roll(
                window, (half - tap) % total_cols, 1
            )
        response = jnp.dot(band_ref[...], patches[member], preferred_element_type=jnp.float32)
        scale = weighting[member] * inverse
        for kernel in range(kernel_total):
            coeffs = [coef_ref[member, kernel, order] for order in range(6)]
            own = response[kernel * out_rows : (kernel + 1) * out_rows]
            factors = (
                coeffs[0] + coeffs[2] * y_coord + coeffs[5] * (y_coord * y_coord),
                coeffs[1] + coeffs[4] * y_coord,
                coeffs[3],
            )
            sums = [
                value + over_columns(factor * scale) * own
                for value, factor in zip(sums, factors, strict=True)
            ]
    coadded = sums[0] + x_coord * (sums[1] + x_coord * sums[2])
    coadd_ref[...] = coadded[:tile_rows, :tile_cols]

    coadded = jnp.where(in_band[:1], coadded, 0.0)
    lead = out_rows - tile_rows - 8
    tall[lead : lead + tile_rows + 16, :] = coadded[: tile_rows + 16]
    tall[:lead, :] = coadded[out_rows - lead :]
    filtered = taps_ref[0] * tall[lead - half : lead - half + tile_rows, :]
    for tap in range(1, side):
        begin = lead - half + tap
        filtered = filtered + taps_ref[tap] * tall[begin : begin + tile_rows, :]
    detection = taps_ref[0] * pltpu.roll(filtered, half, 1)
    for tap in range(1, side):
        detection = detection + taps_ref[tap] * pltpu.roll(filtered, (half - tap) % total_cols, 1)
    detection_ref[...] = detection[:, :tile_cols]


def on_device(
    exposures, basis_kernels, poly_coef, exposure_weight, row_start, row_count, filter_taps
):
    members, tile_rows, tile_cols = exposures.shape
    side = basis_kernels.shape[1]
    half, out_rows, in_rows = sizes(tile_rows, side)
    peers, wide_peers = lax.axis_size("narrow"), lax.axis_size("wide")

    def swapped(array, index):
        return lax.ppermute(array, "narrow", [(i, i ^ index) for i in range(peers)])

    core_pairs = [(i, i ^ 1) for i in range(wide_peers)]
    cross_pairs = [(i, ((i - 1) ^ 1) + 1) for i in range(1, wide_peers - 1)]
    cross_pairs += [(0, wide_peers - 1), (wide_peers - 1, 0)]

    edge_shape = jax.ShapeDtypeStruct((tile_rows, LANES), exposures.dtype)
    to_core, to_cross = pl.pallas_call(
        functools.partial(edges_kernel, 2 * half), out_shape=(edge_shape, edge_shape), name="edges"
    )(exposures)
    from_core = lax.ppermute(to_core, "wide", core_pairs)
    from_cross = lax.ppermute(to_cross, "wide", cross_pairs)
    tiles = [exposures] + [swapped(exposures, index) for index in range(1, peers)]
    both = jnp.stack([from_core, from_cross])
    edges = [both] + [swapped(both, index) for index in range(1, peers)]

    band = band_matrix(basis_kernels, tile_rows)
    depth = band.shape[1]
    total_cols = tile_cols + LANES
    smem = pl.BlockSpec(memory_space=pltpu.SMEM)
    vmem = pl.BlockSpec(memory_space=pltpu.VMEM)
    out = jax.ShapeDtypeStruct((tile_rows, tile_cols), jnp.float32)
    return pl.pallas_call(
        functools.partial(coadd_kernel, peers, wide_peers, side),
        out_shape=(out, out),
        in_specs=[smem] * 5 + [vmem] * (1 + 2 * peers),
        out_specs=(vmem, vmem),
        scratch_shapes=[
            pltpu.VMEM((peers, members, tile_rows, total_cols), jnp.bfloat16),
            pltpu.VMEM((members, depth, total_cols), jnp.bfloat16),
            pltpu.VMEM((out_rows + 8, total_cols), jnp.float32),
        ],
        compiler_params=pltpu.CompilerParams(vmem_limit_bytes=VMEM_BYTES),
        name="coadd",
    )(
        poly_coef,
        exposure_weight,
        row_start,
        row_count,
        filter_taps,
        band,
        *tiles,
        *edges,
    )


def solution(mesh):
    placed = (P(None, "narrow", "wide"), P(), P(), P(), P(), P(), P())
    return jax.shard_map(
        on_device,
        mesh=mesh,
        in_specs=placed,
        out_specs=(P("narrow", "wide"), P("narrow", "wide")),
        check_vma=False,
    )
```

```python
import functools

import jax
import jax.numpy as jnp
from jax import lax
from jax.experimental import pallas as pl
from jax.experimental.pallas import tpu as pltpu
from jax.sharding import PartitionSpec as P

LANES = 128
VMEM_BYTES = 48 << 20


def rounded(value, unit):
    return -(-value // unit) * unit


def sizes(tile_rows, side):
    half = side // 2
    out_rows = rounded(tile_rows + 2 * half, 8)
    in_rows = rounded(tile_rows + 4 * half, 16)
    return half, out_rows, in_rows


def band_matrix_kernel(out_rows, base_ref, band_ref):
    kernel_total, wide = base_ref.shape
    depth = band_ref.shape[1]
    parts = []
    for kernel in range(kernel_total):
        spread = jnp.broadcast_to(base_ref[kernel : kernel + 1, :], (8, wide))
        block = pltpu.roll(spread, 0, 1, stride=1, stride_axis=0)
        parts += [block] + [pltpu.roll(block, first, 1) for first in range(8, out_rows, 8)]
    band_ref[...] = jnp.concatenate(parts, axis=0).astype(jnp.bfloat16)[:, :depth]


def band_matrix(basis_kernels, tile_rows):
    kernel_total, side = basis_kernels.shape[:2]
    half, out_rows, in_rows = sizes(tile_rows, side)
    depth = side * in_rows + 16
    wide = rounded(depth, LANES)
    lead = 32 - 2 * half
    base = basis_kernels.astype(jnp.float32).transpose(0, 2, 1)
    base = jnp.pad(base, ((0, 0), (0, 0), (0, in_rows - side))).reshape(kernel_total, -1)
    base = jnp.pad(base, ((0, 0), (lead, wide - lead - base.shape[1])))
    return pl.pallas_call(
        functools.partial(band_matrix_kernel, out_rows),
        out_shape=jax.ShapeDtypeStruct((kernel_total * out_rows, depth), jnp.bfloat16),
        compiler_params=pltpu.CompilerParams(vmem_limit_bytes=VMEM_BYTES),
        name="band_matrix",
    )(base)


def place_kernel(peers, start_ref, count_ref, *refs):
    tiles = refs[:peers]
    window_ref, core_ref, cross_ref, frame = refs[peers:]
    members, tile_rows, tile_cols = tiles[0].shape
    narrow = lax.axis_index("narrow")
    odd = lax.rem(lax.axis_index("wide"), 2) == 1
    for index in range(peers):
        frame[jnp.bitwise_xor(narrow, index)] = tiles[index][...]
    rows = window_ref.shape[1]
    lane = lax.broadcasted_iota(jnp.int32, (rows, LANES), 1)
    leftward = jnp.zeros((rows, LANES), jnp.bfloat16)
    rightward = jnp.zeros((rows, LANES), jnp.bfloat16)
    for member in range(members):
        slot = narrow - start_ref[member] // tile_rows
        here = jnp.clip(slot, 0, peers - 1)
        above = jnp.clip(slot - 1, 0, peers - 1)
        below = jnp.clip(slot + 1, 0, peers - 1)
        window = jnp.concatenate([frame[above, member], frame[here, member], frame[below, member]])
        frame_row = lax.broadcasted_iota(jnp.int32, window.shape, 0) + (slot - 1) * tile_rows
        present = (frame_row >= 0) & (frame_row < count_ref[member])
        window = jnp.where(present, window, jnp.zeros((), window.dtype))
        window_ref[member] = window
        own = lane // 32 == member
        first = pltpu.roll(window[:, :LANES], 32 * member, 1)
        last = pltpu.roll(window[:, tile_cols - LANES :], (32 * member + 32) % LANES, 1)
        leftward = jnp.where(own, first, leftward)
        rightward = jnp.where(own, last, rightward)

    @pl.when(odd)
    def _():
        core_ref[...] = leftward
        cross_ref[...] = rightward

    @pl.when(jnp.logical_not(odd))
    def _():
        core_ref[...] = rightward
        cross_ref[...] = leftward


def coadd_kernel(
    peers,
    wide_peers,
    side,
    coef_ref,
    weight_ref,
    start_ref,
    count_ref,
    taps_ref,
    band_ref,
    window_ref,
    core_ref,
    cross_ref,
    coadd_ref,
    detection_ref,
    patches,
    tall,
):
    tile_rows, tile_cols = coadd_ref.shape
    members, window_rows = window_ref.shape[:2]
    half, out_rows, in_rows = sizes(tile_rows, side)
    rim = 2 * half
    total_cols = tile_cols + LANES
    kernel_total = band_ref.shape[0] // out_rows
    narrow, wide = lax.axis_index("narrow"), lax.axis_index("wide")
    odd = lax.rem(wide, 2) == 1
    row_base = narrow * tile_rows
    band_rows, band_cols = peers * tile_rows, wide_peers * tile_cols

    edge_lane = lax.broadcasted_iota(jnp.int32, (window_rows, LANES), 1)
    keep_after = (edge_lane < rim) & (wide < wide_peers - 1)
    keep_before = (edge_lane >= LANES - rim) & (wide > 0)
    none = jnp.zeros((window_rows, LANES), jnp.bfloat16)
    after = jnp.where(odd, cross_ref[...], core_ref[...])
    before = jnp.where(odd, core_ref[...], cross_ref[...])

    place = lax.broadcasted_iota(jnp.int32, (out_rows, LANES), 0)
    row = row_base - half + place
    y_coord = (2 * row + 1).astype(jnp.float32) / band_rows - 1.0
    lane = lax.broadcasted_iota(jnp.int32, (8, total_cols), 1)
    column = wide * tile_cols + jnp.where(lane < tile_cols + LANES // 2, lane, lane - total_cols)
    x_coord = ((2 * column + 1).astype(jnp.float32) / band_cols - 1.0)[:1]
    in_band = (column >= 0) & (column < band_cols)
    weighting = []
    for member in range(members):
        inside = (row >= start_ref[member]) & (row < start_ref[member] + count_ref[member])
        weighting.append(jnp.where(inside, weight_ref[member], 0.0))
    denominator = functools.reduce(jnp.add, weighting)
    valid = (row >= 0) & (row < band_rows)
    inverse = jnp.where(valid, 1.0 / jnp.where(valid, denominator, 1.0), 0.0)
    sums = [jnp.zeros((out_rows, total_cols), jnp.float32) for _ in range(3)]

    def over_columns(array):
        return jnp.concatenate([array] * (total_cols // LANES), axis=1)

    for member in range(members):
        right = pltpu.roll(after, (LANES - 32 * member) % LANES, 1)
        left = pltpu.roll(before, (LANES + 96 - 32 * member) % LANES, 1)
        edge = jnp.where(keep_after, right, jnp.where(keep_before, left, none))
        window = jnp.concatenate([window_ref[member], edge], axis=1)
        upper = lax.broadcasted_iota(jnp.int32, (16, total_cols), 0) < 8
        last = jnp.zeros((16, total_cols), jnp.bfloat16)
        for tap in range(side):
            turned = pltpu.roll(window, (half - tap) % total_cols, 1)
            begin = tap * in_rows
            patches[member, begin : begin + 16, :] = jnp.where(upper, last, turned[:16])
            patches[member, begin + 16 : begin + in_rows, :] = turned[16:in_rows]
            last = turned[in_rows:]
        patches[member, side * in_rows :, :] = last
        response = jnp.dot(band_ref[...], patches[member], preferred_element_type=jnp.float32)
        scale = weighting[member] * inverse
        for kernel in range(kernel_total):
            coeffs = [coef_ref[member, kernel, order] for order in range(6)]
            own = response[kernel * out_rows : (kernel + 1) * out_rows]
            factors = (
                coeffs[0] + coeffs[2] * y_coord + coeffs[5] * (y_coord * y_coord),
                coeffs[1] + coeffs[4] * y_coord,
                coeffs[3],
            )
            sums = [
                value + over_columns(factor * scale) * own
                for value, factor in zip(sums, factors, strict=True)
            ]
    coadded = sums[0] + x_coord * (sums[1] + x_coord * sums[2])
    coadded = jnp.where(in_band[:1], coadded, 0.0)
    tall[...] = coadded
    coadd_ref[...] = tall[half : half + tile_rows, :tile_cols]
    filtered = taps_ref[0] * tall[:tile_rows, :]
    for tap in range(1, side):
        filtered = filtered + taps_ref[tap] * tall[tap : tap + tile_rows, :]
    detection = taps_ref[0] * pltpu.roll(filtered, half, 1)
    for tap in range(1, side):
        detection = detection + taps_ref[tap] * pltpu.roll(filtered, (half - tap) % total_cols, 1)
    detection_ref[...] = detection[:, :tile_cols]


def on_device(
    exposures, basis_kernels, poly_coef, exposure_weight, row_start, row_count, filter_taps
):
    members, tile_rows, tile_cols = exposures.shape
    side = basis_kernels.shape[1]
    half, out_rows, in_rows = sizes(tile_rows, side)
    peers, wide_peers = lax.axis_size("narrow"), lax.axis_size("wide")
    smem = pl.BlockSpec(memory_space=pltpu.SMEM)
    vmem = pl.BlockSpec(memory_space=pltpu.VMEM)

    def swapped(array, index):
        return lax.ppermute(array, "narrow", [(i, i ^ index) for i in range(peers)])

    tiles = [exposures] + [swapped(exposures, index) for index in range(1, peers)]
    band = band_matrix(basis_kernels, tile_rows)
    depth = band.shape[1]
    window_rows = 3 * tile_rows
    edge_shape = jax.ShapeDtypeStruct((window_rows, LANES), exposures.dtype)
    window_shape = jax.ShapeDtypeStruct((members, window_rows, tile_cols), exposures.dtype)
    window, to_core, to_cross = pl.pallas_call(
        functools.partial(place_kernel, peers),
        out_shape=(window_shape, edge_shape, edge_shape),
        in_specs=[smem] * 2 + [vmem] * peers,
        out_specs=[vmem] * 3,
        scratch_shapes=[pltpu.VMEM((peers, members, tile_rows, tile_cols), jnp.bfloat16)],
        compiler_params=pltpu.CompilerParams(vmem_limit_bytes=VMEM_BYTES),
        name="place",
    )(row_start, row_count, *tiles)
    core_pairs = [(i, i ^ 1) for i in range(wide_peers)]
    cross_pairs = [(i, ((i - 1) ^ 1) + 1) for i in range(1, wide_peers - 1)]
    cross_pairs += [(0, wide_peers - 1), (wide_peers - 1, 0)]
    from_core = lax.ppermute(to_core, "wide", core_pairs)
    from_cross = lax.ppermute(to_cross, "wide", cross_pairs)

    total_cols = tile_cols + LANES
    out = jax.ShapeDtypeStruct((tile_rows, tile_cols), jnp.float32)
    return pl.pallas_call(
        functools.partial(coadd_kernel, peers, wide_peers, side),
        out_shape=(out, out),
        in_specs=[smem] * 5 + [vmem] * 4,
        out_specs=(vmem, vmem),
        scratch_shapes=[
            pltpu.VMEM((members, depth, total_cols), jnp.bfloat16),
            pltpu.VMEM((out_rows, total_cols), jnp.float32),
        ],
        compiler_params=pltpu.CompilerParams(vmem_limit_bytes=VMEM_BYTES),
        name="coadd",
    )(
        poly_coef,
        exposure_weight,
        row_start,
        row_count,
        filter_taps,
        band,
        window,
        from_core,
        from_cross,
    )


def solution(mesh):
    placed = (P(None, "narrow", "wide"), P(), P(), P(), P(), P(), P())
    return jax.shard_map(
        on_device,
        mesh=mesh,
        in_specs=placed,
        out_specs=(P("narrow", "wide"), P("narrow", "wide")),
        check_vma=False,
    )
```

```python
import functools

import jax
import jax.numpy as jnp
from jax import lax
from jax.experimental import pallas as pl
from jax.experimental.pallas import tpu as pltpu
from jax.sharding import PartitionSpec as P

LANES = 128
VMEM_BYTES = 48 << 20


def rounded(value, unit):
    return -(-value // unit) * unit


def sizes(tile_rows, side):
    half = side // 2
    out_rows = rounded(tile_rows + 2 * half, 8)
    in_rows = rounded(tile_rows + 4 * half, 16)
    return half, out_rows, in_rows


def band_matrix_kernel(half, out_rows, in_rows, base_ref, band_ref):
    kernel_total, wide = base_ref.shape
    depth = band_ref.shape[1]
    place = lax.rem(lax.broadcasted_iota(jnp.int32, (8, wide), 1), in_rows)
    below = place < in_rows - 24
    parts = []
    for kernel in range(kernel_total):
        spread = jnp.broadcast_to(base_ref[kernel : kernel + 1, :], (8, wide))
        block = pltpu.roll(spread, 0, 1, stride=1, stride_axis=0)
        for first in range(0, out_rows, 8):
            shift = first - 2 * half
            plain = pltpu.roll(block, shift % wide, 1)
            wrapped = pltpu.roll(block, (shift + in_rows) % wide, 1)
            parts.append(jnp.where(below, plain, wrapped))
    band_ref[...] = jnp.concatenate(parts, axis=0).astype(jnp.bfloat16)[:, :depth]


def band_matrix(basis_kernels, tile_rows):
    kernel_total, side = basis_kernels.shape[:2]
    half, out_rows, in_rows = sizes(tile_rows, side)
    depth = side * in_rows
    wide = rounded(depth, LANES)
    base = basis_kernels.astype(jnp.float32).transpose(0, 2, 1)
    base = jnp.pad(base, ((0, 0), (0, 0), (0, in_rows - side))).reshape(kernel_total, depth)
    base = jnp.pad(base, ((0, 0), (0, wide - depth)))
    return pl.pallas_call(
        functools.partial(band_matrix_kernel, half, out_rows, in_rows),
        out_shape=jax.ShapeDtypeStruct((kernel_total * out_rows, depth), jnp.bfloat16),
        compiler_params=pltpu.CompilerParams(vmem_limit_bytes=VMEM_BYTES),
        cost_estimate=pl.CostEstimate(flops=10**9, bytes_accessed=10**6, transcendentals=0),
        name="band_matrix",
    )(base)


def place_kernel(sent, start_ref, count_ref, band_ref, *refs):
    peers = len(sent)
    tiles = refs[:peers][::-1]
    window_ref, core_ref, cross_ref, frame = refs[peers:]
    members, window_rows, tile_cols = window_ref.shape
    tile_rows = tiles[0].shape[1]
    narrow = lax.axis_index("narrow")
    odd = lax.rem(lax.axis_index("wide"), 2) == 1
    for index in range(peers):
        frame[jnp.bitwise_xor(narrow, index), sent[index] :] = tiles[index][...]
    lane = lax.broadcasted_iota(jnp.int32, (window_rows, LANES), 1)
    upper = lax.broadcasted_iota(jnp.int32, (16, tile_cols), 0) < 8
    leftward = jnp.zeros((window_rows, LANES), jnp.bfloat16)
    rightward = jnp.zeros((window_rows, LANES), jnp.bfloat16)
    for member in range(members):
        slot = narrow - start_ref[member] // tile_rows
        here = jnp.clip(slot, 0, peers - 1)
        above = jnp.clip(slot - 1, 0, peers - 1)
        below = jnp.clip(slot + 1, 0, peers - 1)
        window = jnp.concatenate(
            [
                frame[here, member],
                frame[below, member, :16],
                jnp.where(upper, frame[below, member, 16:], frame[above, member, :16]),
                frame[above, member, 16:],
            ]
        )
        place = lax.broadcasted_iota(jnp.int32, window.shape, 0)
        offset = jnp.where(place < window_rows - 24, place, place - window_rows)
        frame_row = offset + slot * tile_rows
        present = (frame_row >= 0) & (frame_row < count_ref[member])
        window = jnp.where(present, window, jnp.zeros((), window.dtype))
        window_ref[member] = window
        own = lane // 32 == member
        first = pltpu.roll(window[:, :LANES], 32 * member, 1)
        last = pltpu.roll(window[:, tile_cols - LANES :], (32 * member + 32) % LANES, 1)
        leftward = jnp.where(own, first, leftward)
        rightward = jnp.where(own, last, rightward)

    @pl.when(odd)
    def _():
        core_ref[...] = leftward
        cross_ref[...] = rightward

    @pl.when(jnp.logical_not(odd))
    def _():
        core_ref[...] = rightward
        cross_ref[...] = leftward


def row_factors(tile_rows, band_rows, half, out_rows, kernel_total, scalars):
    coef_ref, weight_ref, start_ref, count_ref = scalars
    members = weight_ref.shape[0]
    place = lax.broadcasted_iota(jnp.int32, (out_rows, LANES), 0)
    row = lax.axis_index("narrow") * tile_rows - half + place
    y_coord = (2 * row + 1).astype(jnp.float32) / band_rows - 1.0
    weighting = []
    for member in range(members):
        inside = (row >= start_ref[member]) & (row < start_ref[member] + count_ref[member])
        weighting.append(jnp.where(inside, weight_ref[member], 0.0))
    denominator = functools.reduce(jnp.add, weighting)
    valid = (row >= 0) & (row < band_rows)
    inverse = jnp.where(valid, 1.0 / jnp.where(valid, denominator, 1.0), 0.0)

    def factors(member, kernel):
        coeffs = [coef_ref[member, kernel, order] for order in range(6)]
        scale = weighting[member] * inverse
        return (
            (coeffs[0] + coeffs[2] * y_coord + coeffs[5] * (y_coord * y_coord)) * scale,
            (coeffs[1] + coeffs[4] * y_coord) * scale,
            coeffs[3] * scale,
        )

    return factors


def column_position(column, band_cols):
    return (2 * column + 1).astype(jnp.float32) / band_cols - 1.0


def main_kernel(
    peers, wide_peers, side, tile_rows, coef_ref, weight_ref, start_ref, count_ref, band_ref, window_ref, out_ref, patches
):
    members, in_rows, tile_cols = window_ref.shape
    half, out_rows, _ = sizes(tile_rows, side)
    kernel_total = band_ref.shape[0] // out_rows
    scalars = (coef_ref, weight_ref, start_ref, count_ref)
    factors = row_factors(tile_rows, peers * tile_rows, half, out_rows, kernel_total, scalars)
    sums = [jnp.zeros((out_rows, tile_cols), jnp.float32) for _ in range(3)]
    group = patches.shape[2] // tile_cols
    for begin in range(0, members, group):
        for member in range(begin, begin + group):
            window = window_ref[member]
            lanes = slice((member - begin) * tile_cols, (member - begin + 1) * tile_cols)
            for tap in range(side):
                patches[begin // group, tap * in_rows : (tap + 1) * in_rows, lanes] = pltpu.roll(
                    window, (half - tap) % tile_cols, 1
                )
        responses = jnp.dot(
            band_ref[...], patches[begin // group], preferred_element_type=jnp.float32
        )
        for member in range(begin, begin + group):
            response = responses[:, (member - begin) * tile_cols : (member - begin + 1) * tile_cols]
            for kernel in range(kernel_total):
                own = response[kernel * out_rows : (kernel + 1) * out_rows]
                sums = [
                    value + jnp.concatenate([factor] * (tile_cols // LANES), axis=1) * own
                    for value, factor in zip(sums, factors(member, kernel), strict=True)
                ]
    column = lax.axis_index("wide") * tile_cols + lax.broadcasted_iota(
        jnp.int32, (8, tile_cols), 1
    )
    x_coord = column_position(column, wide_peers * tile_cols)[:1]
    out_ref[...] = sums[0] + x_coord * (sums[1] + x_coord * sums[2])


def rim_kernel(
    peers,
    wide_peers,
    side,
    coef_ref,
    weight_ref,
    start_ref,
    count_ref,
    taps_ref,
    band_ref,
    inner_ref,
    to_core_ref,
    to_cross_ref,
    from_core_ref,
    from_cross_ref,
    coadd_ref,
    detection_ref,
    patches,
    tall,
):
    tile_rows, tile_cols = coadd_ref.shape
    in_rows = to_core_ref.shape[0]
    members = weight_ref.shape[0]
    half, out_rows, _ = sizes(tile_rows, side)
    rim = 2 * half
    kernel_total = band_ref.shape[0] // out_rows
    band_cols = wide_peers * tile_cols
    wide = lax.axis_index("wide")
    odd = lax.rem(wide, 2) == 1
    scalars = (coef_ref, weight_ref, start_ref, count_ref)
    factors = row_factors(tile_rows, peers * tile_rows, half, out_rows, kernel_total, scalars)

    none = jnp.zeros((in_rows, LANES), jnp.bfloat16)
    core, cross = from_core_ref[...], from_cross_ref[...]
    before = jnp.where(wide > 0, jnp.where(odd, core, cross), none)
    after = jnp.where(wide < wide_peers - 1, jnp.where(odd, cross, core), none)
    first = jnp.where(odd, to_core_ref[...], to_cross_ref[...])
    last = jnp.where(odd, to_cross_ref[...], to_core_ref[...])
    lane = lax.broadcasted_iota(jnp.int32, (in_rows, LANES), 1)
    zones = []
    for member in range(members):
        pieces = [
            pltpu.roll(piece, (target - 32 * member) % LANES, 1)
            for piece, target in ((before, -12), (first, rim), (last, 2 * rim - 12), (after, 3 * rim))
        ]
        zone = none
        for index in reversed(range(4)):
            zone = jnp.where(lane < (index + 1) * rim, pieces[index], zone)
        zones.append(zone)
    zones = jnp.concatenate(zones, axis=1)
    for tap in range(side):
        patches[tap * in_rows : (tap + 1) * in_rows, :] = pltpu.roll(
            zones, (half - tap) % zones.shape[1], 1
        )
    response = jnp.dot(band_ref[...], patches[...], preferred_element_type=jnp.float32)
    sums = [jnp.zeros((out_rows, LANES), jnp.float32) for _ in range(3)]
    for member in range(members):
        for kernel in range(kernel_total):
            own = response[
                kernel * out_rows : (kernel + 1) * out_rows, member * LANES : (member + 1) * LANES
            ]
            sums = [
                value + factor * own
                for value, factor in zip(sums, factors(member, kernel), strict=True)
            ]
    lane = lax.broadcasted_iota(jnp.int32, (out_rows, LANES), 1)
    column = wide * tile_cols + jnp.where(lane < 2 * rim, lane - rim, tile_cols - 3 * rim + lane)
    x_coord = column_position(column, band_cols)
    border = sums[0] + x_coord * (sums[1] + x_coord * sums[2])
    border = jnp.where((column >= 0) & (column < band_cols), border, 0.0)

    width = tile_cols + LANES
    head = pltpu.roll(border, LANES - rim, 1)
    tail = pltpu.roll(border, LANES - 3 * rim, 1)
    left = pltpu.roll(border, LANES - rim, 1)
    right = pltpu.roll(border, LANES - 3 * rim, 1)
    tall[:, :LANES] = jnp.where(lane < half, head, inner_ref[:, :LANES])
    tall[:, LANES : tile_cols - LANES] = inner_ref[:, LANES : tile_cols - LANES]
    tall[:, tile_cols - LANES : tile_cols] = jnp.where(
        lane >= LANES - half, tail, inner_ref[:, tile_cols - LANES :]
    )
    tall[:, tile_cols:] = jnp.where(lane < LANES // 2, right, left)
    coadd_ref[...] = tall[half : half + tile_rows, :tile_cols]
    filtered = taps_ref[0] * tall[:tile_rows, :]
    for tap in range(1, side):
        filtered = filtered + taps_ref[tap] * tall[tap : tap + tile_rows, :]
    detection = taps_ref[0] * pltpu.roll(filtered, half, 1)
    for tap in range(1, side):
        detection = detection + taps_ref[tap] * pltpu.roll(filtered, (half - tap) % width, 1)
    detection_ref[...] = detection[:, :tile_cols]


def on_device(
    exposures, basis_kernels, poly_coef, exposure_weight, row_start, row_count, filter_taps
):
    members, tile_rows, tile_cols = exposures.shape
    side = basis_kernels.shape[1]
    half, out_rows, in_rows = sizes(tile_rows, side)
    peers, wide_peers = lax.axis_size("narrow"), lax.axis_size("wide")
    smem = pl.BlockSpec(memory_space=pltpu.SMEM)
    vmem = pl.BlockSpec(memory_space=pltpu.VMEM)
    params = pltpu.CompilerParams(vmem_limit_bytes=VMEM_BYTES)

    def skipped(index):
        return 0 if any(abs(i - (i ^ index)) <= 1 for i in range(peers)) else 1

    sent = [skipped(index) for index in range(peers)]
    tiles = [exposures] * peers
    for index in reversed(range(1, peers)):
        pairs = [(i, i ^ index) for i in range(peers)]
        tiles[index] = lax.ppermute(exposures[sent[index] :], "narrow", pairs)
    band = band_matrix(basis_kernels, tile_rows)
    depth = band.shape[1]
    edge_shape = jax.ShapeDtypeStruct((in_rows, LANES), exposures.dtype)
    window_shape = jax.ShapeDtypeStruct((members, in_rows, tile_cols), exposures.dtype)
    window, to_core, to_cross = pl.pallas_call(
        functools.partial(place_kernel, sent),
        out_shape=(window_shape, edge_shape, edge_shape),
        in_specs=[smem] * 2 + [pl.BlockSpec(memory_space=pl.ANY)] + [vmem] * peers,
        out_specs=[vmem] * 3,
        scratch_shapes=[pltpu.VMEM((peers, members, tile_rows, tile_cols), jnp.bfloat16)],
        compiler_params=params,
        name="place",
    )(row_start, row_count, band, *reversed(tiles))
    core_pairs = [(i, i ^ 1) for i in range(wide_peers)]
    cross_pairs = [(i, ((i - 1) ^ 1) + 1) for i in range(1, wide_peers - 1)]
    cross_pairs += [(0, wide_peers - 1), (wide_peers - 1, 0)]
    from_core = lax.ppermute(to_core, "wide", core_pairs)
    from_cross = lax.ppermute(to_cross, "wide", cross_pairs)

    scalars = (poly_coef, exposure_weight, row_start, row_count)
    inner = pl.pallas_call(
        functools.partial(main_kernel, peers, wide_peers, side, tile_rows),
        out_shape=jax.ShapeDtypeStruct((out_rows, tile_cols), jnp.float32),
        in_specs=[smem] * 4 + [vmem] * 2,
        out_specs=vmem,
        scratch_shapes=[pltpu.VMEM((members // 2, depth, 2 * tile_cols), jnp.bfloat16)],
        compiler_params=params,
        cost_estimate=pl.CostEstimate(flops=2 * 10**9, bytes_accessed=10**6, transcendentals=0),
        name="main",
    )(*scalars, band, window)
    out = jax.ShapeDtypeStruct((tile_rows, tile_cols), jnp.float32)
    return pl.pallas_call(
        functools.partial(rim_kernel, peers, wide_peers, side),
        out_shape=(out, out),
        in_specs=[smem] * 5 + [vmem] * 6,
        out_specs=(vmem, vmem),
        scratch_shapes=[
            pltpu.VMEM((depth, members * LANES), jnp.bfloat16),
            pltpu.VMEM((out_rows, tile_cols + LANES), jnp.float32),
        ],
        compiler_params=params,
        name="rim",
    )(*scalars, filter_taps, band, inner, to_core, to_cross, from_core, from_cross)


def solution(mesh):
    placed = (P(None, "narrow", "wide"), P(), P(), P(), P(), P(), P())
    return jax.shard_map(
        on_device,
        mesh=mesh,
        in_specs=placed,
        out_specs=(P("narrow", "wide"), P("narrow", "wide")),
        check_vma=False,
    )
```

```python
import functools

import jax
import jax.numpy as jnp
from jax import lax
from jax.experimental import pallas as pl
from jax.experimental.pallas import tpu as pltpu
from jax.sharding import PartitionSpec as P

LANES = 128
VMEM_BYTES = 48 << 20


def rounded(value, unit):
    return -(-value // unit) * unit


def sizes(tile_rows, side):
    half = side // 2
    out_rows = rounded(tile_rows + 2 * half, 8)
    in_rows = rounded(tile_rows + 4 * half, 16)
    return half, out_rows, in_rows


UPPER = 24
PART = 48


def band_matrix(half, begin, base, band_ref):
    kernel_total, wide = len(base), base[0].shape[1]
    rows, depth = band_ref.shape
    place = lax.rem(lax.broadcasted_iota(jnp.int32, (8, wide), 1), PART)
    lead = begin - 2 * half
    parts = []
    for kernel in range(kernel_total):
        spread = jnp.broadcast_to(base[kernel], (8, wide))
        block = pltpu.roll(spread, 0, 1, stride=1, stride_axis=0)
        for first in range(0, rows // kernel_total, 8):
            shift = first + lead
            plain = pltpu.roll(block, shift % wide, 1)
            wrapped = pltpu.roll(block, (shift + (PART if lead < 0 else -PART)) % wide, 1)
            if lead < 0:
                parts.append(jnp.where(place < PART + lead - 4, plain, wrapped))
            else:
                parts.append(jnp.where(place < lead, wrapped, plain))
    band_ref[...] = jnp.concatenate(parts, axis=0).astype(jnp.bfloat16)[:, :depth]


def factors_kernel(
    tile_rows, band_rows, half, coef_ref, weight_ref, start_ref, count_ref, after_ref, factor_ref
):
    kernel_total, members = coef_ref.shape[:2]
    out_rows = factor_ref.shape[1]
    place = lax.broadcasted_iota(jnp.int32, (out_rows, LANES), 0)
    row = lax.axis_index("narrow") * tile_rows - half + place
    y_coord = (2 * row + 1).astype(jnp.float32) / band_rows - 1.0
    weighting = []
    for member in range(members):
        inside = (row >= start_ref[member]) & (row < start_ref[member] + count_ref[member])
        weighting.append(jnp.where(inside, weight_ref[member], 0.0))
    denominator = functools.reduce(jnp.add, weighting)
    valid = (row >= 0) & (row < band_rows)
    inverse = jnp.where(valid, 1.0 / jnp.where(valid, denominator, 1.0), 0.0)
    for member in range(members):
        scale = weighting[member] * inverse
        for kernel in range(kernel_total):
            coeffs = [coef_ref[kernel, member, order] for order in range(6)]
            constant = coeffs[0] + coeffs[2] * y_coord + coeffs[5] * (y_coord * y_coord)
            index = 3 * (member * kernel_total + kernel)
            factor_ref[index] = constant * scale
            factor_ref[index + 1] = (coeffs[1] + coeffs[4] * y_coord) * scale
            factor_ref[index + 2] = coeffs[3] * scale


def spread_taps(basis_ref, square):
    kernel_total, side = basis_ref.shape[:2]
    rows = square.shape[0] // kernel_total
    wide = rounded(side * PART, LANES)
    square[...] = jnp.zeros_like(square)
    for kernel in range(kernel_total):
        square[kernel * rows : kernel * rows + side, :side] = basis_ref[kernel].astype(jnp.float32)
    across = lax.broadcasted_iota(jnp.int32, (LANES, wide), 0)
    begin = across * PART
    lane = lax.broadcasted_iota(jnp.int32, (LANES, wide), 1)
    onehot = jnp.where((lane >= begin) & (lane < begin + PART), 1.0, 0.0).astype(jnp.bfloat16)
    repeated = jnp.dot(
        square[...].astype(jnp.bfloat16), onehot, preferred_element_type=jnp.float32
    )
    down = lax.broadcasted_iota(jnp.int32, (rows, wide), 0)
    chosen = lax.rem(lax.broadcasted_iota(jnp.int32, (rows, wide), 1), PART) == down
    return [
        jnp.sum(
            jnp.where(chosen, repeated[kernel * rows : (kernel + 1) * rows], 0.0),
            axis=0,
            keepdims=True,
        )
        for kernel in range(kernel_total)
    ]


def bands_kernel(half, basis_ref, upper_ref, lower_ref, square):
    base = spread_taps(basis_ref, square)
    band_matrix(half, 0, base, upper_ref)
    band_matrix(half, UPPER, base, lower_ref)


def prepared(basis_kernels, poly_coef, weight, start, count, tile_rows):
    kernel_total, side = basis_kernels.shape[:2]
    members = poly_coef.shape[0]
    half, out_rows, _ = sizes(tile_rows, side)
    depth = side * PART
    smem = pl.BlockSpec(memory_space=pltpu.SMEM)
    vmem = pl.BlockSpec(memory_space=pltpu.VMEM)
    params = pltpu.CompilerParams(vmem_limit_bytes=VMEM_BYTES)
    band_rows = lax.axis_size("narrow") * tile_rows
    upper, lower = pl.pallas_call(
        functools.partial(bands_kernel, half),
        out_shape=(
            jax.ShapeDtypeStruct((kernel_total * UPPER, depth), jnp.bfloat16),
            jax.ShapeDtypeStruct((kernel_total * (out_rows - UPPER), depth), jnp.bfloat16),
        ),
        in_specs=[vmem],
        out_specs=(vmem, vmem),
        scratch_shapes=[pltpu.VMEM((kernel_total * rounded(side, 8), LANES), jnp.float32)],
        compiler_params=params,
        cost_estimate=pl.CostEstimate(flops=10**9, bytes_accessed=10**6, transcendentals=0),
        name="bands",
    )(basis_kernels)
    factors = pl.pallas_call(
        functools.partial(factors_kernel, tile_rows, band_rows, half),
        out_shape=jax.ShapeDtypeStruct((3 * members * kernel_total, out_rows, LANES), jnp.float32),
        in_specs=[smem] * 4 + [pl.BlockSpec(memory_space=pl.ANY)],
        out_specs=vmem,
        compiler_params=params,
        cost_estimate=pl.CostEstimate(flops=10**8, bytes_accessed=10**6, transcendentals=0),
        name="factors",
    )(poly_coef.transpose(1, 0, 2), weight, start, count, upper)
    return factors, upper, lower


def part_rows_of(moved):
    first, second, below, mixed, above = [moved[row : row + 16] for row in range(0, 80, 16)]
    place = lax.broadcasted_iota(jnp.int32, first.shape, 0)
    return (
        (first, jnp.where(place < 8, second, mixed), above),
        (jnp.where(place < 4, mixed, first), second, below),
    )


def fill_patches(window, half, side, patch_refs, lanes):
    width = window.shape[1]
    for tap in range(side):
        moved = pltpu.roll(window, (half - tap) % width, 1)
        for patch_ref, rows in zip(patch_refs, part_rows_of(moved), strict=True):
            for index, piece in enumerate(rows):
                begin = tap * PART + 16 * index
                patch_ref[begin : begin + 16, lanes] = piece


def products(band_refs, patch_refs):
    return [
        jnp.dot(band_ref[...], patch_ref[...], preferred_element_type=jnp.float32)
        for band_ref, patch_ref in zip(band_refs, patch_refs, strict=True)
    ]


def response_of(parts, kernel, kernel_total, lanes):
    pieces = []
    for part in parts:
        rows = part.shape[0] // kernel_total
        pieces.append(part[kernel * rows : (kernel + 1) * rows, lanes])
    return jnp.concatenate(pieces, axis=0)


def place_kernel(sent, start_ref, count_ref, *refs):
    peers = len(sent)
    tiles = refs[:peers][::-1]
    window_ref, core_ref, cross_ref, frame = refs[peers:]
    members, window_rows, tile_cols = window_ref.shape
    tile_rows = tiles[0].shape[1]
    narrow = lax.axis_index("narrow")
    odd = lax.rem(lax.axis_index("wide"), 2) == 1
    for index in range(peers):
        frame[jnp.bitwise_xor(narrow, index), sent[index] :] = tiles[index][...]
    lane = lax.broadcasted_iota(jnp.int32, (window_rows, LANES), 1)
    upper = lax.broadcasted_iota(jnp.int32, (16, tile_cols), 0) < 8
    leftward = jnp.zeros((window_rows, LANES), jnp.bfloat16)
    rightward = jnp.zeros((window_rows, LANES), jnp.bfloat16)
    for member in range(members):
        slot = narrow - start_ref[member] // tile_rows
        here = jnp.clip(slot, 0, peers - 1)
        above = jnp.clip(slot - 1, 0, peers - 1)
        below = jnp.clip(slot + 1, 0, peers - 1)
        window = jnp.concatenate(
            [
                frame[here, member],
                frame[below, member, :16],
                jnp.where(upper, frame[below, member, 16:], frame[above, member, :16]),
                frame[above, member, 16:],
            ]
        )
        place = lax.broadcasted_iota(jnp.int32, window.shape, 0)
        offset = jnp.where(place < window_rows - 24, place, place - window_rows)
        frame_row = offset + slot * tile_rows
        present = (frame_row >= 0) & (frame_row < count_ref[member])
        window = jnp.where(present, window, jnp.zeros((), window.dtype))
        window_ref[member] = window
        own = lane // 32 == member
        first = pltpu.roll(window[:, :LANES], 32 * member, 1)
        last = pltpu.roll(window[:, tile_cols - LANES :], (32 * member + 32) % LANES, 1)
        leftward = jnp.where(own, first, leftward)
        rightward = jnp.where(own, last, rightward)

    @pl.when(odd)
    def _():
        core_ref[...] = leftward
        cross_ref[...] = rightward

    @pl.when(jnp.logical_not(odd))
    def _():
        core_ref[...] = rightward
        cross_ref[...] = leftward


def column_position(column, band_cols):
    return (2 * column + 1).astype(jnp.float32) / band_cols - 1.0


def main_kernel(
    wide_peers,
    side,
    tile_rows,
    factor_ref,
    upper_ref,
    lower_ref,
    window_ref,
    out_ref,
    upper_patches,
    lower_patches,
):
    members, in_rows, tile_cols = window_ref.shape
    half, out_rows, _ = sizes(tile_rows, side)
    kernel_total = upper_ref.shape[0] // UPPER
    sums = [jnp.zeros((out_rows, tile_cols), jnp.float32) for _ in range(3)]
    group = upper_patches.shape[2] // tile_cols
    for begin in range(0, members, group):
        patch_refs = upper_patches.at[begin // group], lower_patches.at[begin // group]
        strips = [slice(index * tile_cols, (index + 1) * tile_cols) for index in range(group)]
        for index, lanes in enumerate(strips):
            fill_patches(window_ref[begin + index], half, side, patch_refs, lanes)
        parts = products((upper_ref, lower_ref), patch_refs)
        for index, lanes in enumerate(strips):
            for kernel in range(kernel_total):
                own = response_of(parts, kernel, kernel_total, lanes)
                place = 3 * ((begin + index) * kernel_total + kernel)
                for order in range(3):
                    factor = [factor_ref[place + order]] * (tile_cols // LANES)
                    sums[order] = sums[order] + jnp.concatenate(factor, axis=1) * own
    column = lax.axis_index("wide") * tile_cols + lax.broadcasted_iota(
        jnp.int32, (8, tile_cols), 1
    )
    x_coord = column_position(column, wide_peers * tile_cols)[:1]
    out_ref[...] = sums[0] + x_coord * (sums[1] + x_coord * sums[2])


def rim_kernel(
    wide_peers,
    side,
    members,
    taps_ref,
    factor_ref,
    upper_ref,
    lower_ref,
    inner_ref,
    to_core_ref,
    to_cross_ref,
    from_core_ref,
    from_cross_ref,
    coadd_ref,
    detection_ref,
    upper_patches,
    lower_patches,
    tall,
):
    tile_rows, tile_cols = coadd_ref.shape
    in_rows = to_core_ref.shape[0]
    half, out_rows, _ = sizes(tile_rows, side)
    rim = 2 * half
    kernel_total = upper_ref.shape[0] // UPPER
    band_cols = wide_peers * tile_cols
    wide = lax.axis_index("wide")
    odd = lax.rem(wide, 2) == 1

    none = jnp.zeros((in_rows, LANES), jnp.bfloat16)
    core, cross = from_core_ref[...], from_cross_ref[...]
    before = jnp.where(wide > 0, jnp.where(odd, core, cross), none)
    after = jnp.where(wide < wide_peers - 1, jnp.where(odd, cross, core), none)
    first = jnp.where(odd, to_core_ref[...], to_cross_ref[...])
    last = jnp.where(odd, to_cross_ref[...], to_core_ref[...])
    lane = lax.broadcasted_iota(jnp.int32, (in_rows, LANES), 1)
    zones = []
    for member in range(members):
        pieces = [
            pltpu.roll(piece, (target - 32 * member) % LANES, 1)
            for piece, target in ((before, -12), (first, rim), (last, 2 * rim - 12), (after, 3 * rim))
        ]
        zone = none
        for index in reversed(range(4)):
            zone = jnp.where(lane < (index + 1) * rim, pieces[index], zone)
        zones.append(zone)
    zones = jnp.concatenate(zones, axis=1)
    patch_refs = upper_patches, lower_patches
    fill_patches(zones, half, side, patch_refs, slice(0, members * LANES))
    parts = products((upper_ref, lower_ref), patch_refs)
    sums = [jnp.zeros((out_rows, LANES), jnp.float32) for _ in range(3)]
    for member in range(members):
        for kernel in range(kernel_total):
            lanes = slice(member * LANES, (member + 1) * LANES)
            own = response_of(parts, kernel, kernel_total, lanes)
            place = 3 * (member * kernel_total + kernel)
            for order in range(3):
                sums[order] = sums[order] + factor_ref[place + order] * own
    lane = lax.broadcasted_iota(jnp.int32, (out_rows, LANES), 1)
    column = wide * tile_cols + jnp.where(lane < 2 * rim, lane - rim, tile_cols - 3 * rim + lane)
    x_coord = column_position(column, band_cols)
    border = sums[0] + x_coord * (sums[1] + x_coord * sums[2])
    border = jnp.where((column >= 0) & (column < band_cols), border, 0.0)

    width = tile_cols + LANES
    head = pltpu.roll(border, LANES - rim, 1)
    tail = pltpu.roll(border, LANES - 3 * rim, 1)
    left = pltpu.roll(border, LANES - rim, 1)
    right = pltpu.roll(border, LANES - 3 * rim, 1)
    tall[:, :LANES] = jnp.where(lane < half, head, inner_ref[:, :LANES])
    tall[:, LANES : tile_cols - LANES] = inner_ref[:, LANES : tile_cols - LANES]
    tall[:, tile_cols - LANES : tile_cols] = jnp.where(
        lane >= LANES - half, tail, inner_ref[:, tile_cols - LANES :]
    )
    tall[:, tile_cols:] = jnp.where(lane < LANES // 2, right, left)
    coadd_ref[...] = tall[half : half + tile_rows, :tile_cols]
    filtered = taps_ref[0] * tall[:tile_rows, :]
    for tap in range(1, side):
        filtered = filtered + taps_ref[tap] * tall[tap : tap + tile_rows, :]
    detection = taps_ref[0] * pltpu.roll(filtered, half, 1)
    for tap in range(1, side):
        detection = detection + taps_ref[tap] * pltpu.roll(filtered, (half - tap) % width, 1)
    detection_ref[...] = detection[:, :tile_cols]


def on_device(
    exposures, basis_kernels, poly_coef, exposure_weight, row_start, row_count, filter_taps
):
    members, tile_rows, tile_cols = exposures.shape
    side = basis_kernels.shape[1]
    half, out_rows, in_rows = sizes(tile_rows, side)
    peers, wide_peers = lax.axis_size("narrow"), lax.axis_size("wide")
    smem = pl.BlockSpec(memory_space=pltpu.SMEM)
    vmem = pl.BlockSpec(memory_space=pltpu.VMEM)
    params = pltpu.CompilerParams(vmem_limit_bytes=VMEM_BYTES)

    def skipped(index):
        return 0 if any(abs(i - (i ^ index)) <= 1 for i in range(peers)) else 1

    sent = [skipped(index) for index in range(peers)]
    tiles = [exposures] * peers
    moving, latter = lax.optimization_barrier((exposures, exposures[1:]))
    for index in reversed(range(1, peers)):
        pairs = [(i, i ^ index) for i in range(peers)]
        whole = moving if index == 1 else exposures
        tiles[index] = lax.ppermute(latter if sent[index] else whole, "narrow", pairs)
    tables = prepared(
        basis_kernels, poly_coef, exposure_weight, row_start, row_count, tile_rows
    )
    depth = side * PART
    edge_shape = jax.ShapeDtypeStruct((in_rows, LANES), exposures.dtype)
    window_shape = jax.ShapeDtypeStruct((members, in_rows, tile_cols), exposures.dtype)
    window, to_core, to_cross = pl.pallas_call(
        functools.partial(place_kernel, sent),
        out_shape=(window_shape, edge_shape, edge_shape),
        in_specs=[smem] * 2 + [vmem] * peers,
        out_specs=[vmem] * 3,
        scratch_shapes=[pltpu.VMEM((peers, members, tile_rows, tile_cols), jnp.bfloat16)],
        compiler_params=params,
        name="place",
    )(row_start, row_count, *reversed(tiles))
    core_pairs = [(i, i ^ 1) for i in range(wide_peers)]
    cross_pairs = [(i, ((i - 1) ^ 1) + 1) for i in range(1, wide_peers - 1)]
    cross_pairs += [(0, wide_peers - 1), (wide_peers - 1, 0)]
    from_core = lax.ppermute(to_core, "wide", core_pairs)
    from_cross = lax.ppermute(to_cross, "wide", cross_pairs)

    inner = pl.pallas_call(
        functools.partial(main_kernel, wide_peers, side, tile_rows),
        out_shape=jax.ShapeDtypeStruct((out_rows, tile_cols), jnp.float32),
        in_specs=[vmem] * 4,
        out_specs=vmem,
        scratch_shapes=[pltpu.VMEM((members // 2, depth, 2 * tile_cols), jnp.bfloat16)] * 2,
        compiler_params=params,
        cost_estimate=pl.CostEstimate(flops=2 * 10**9, bytes_accessed=10**6, transcendentals=0),
        name="main",
    )(*tables, window)
    out = jax.ShapeDtypeStruct((tile_rows, tile_cols), jnp.float32)
    return pl.pallas_call(
        functools.partial(rim_kernel, wide_peers, side, members),
        out_shape=(out, out),
        in_specs=[smem] + [vmem] * 8,
        out_specs=(vmem, vmem),
        scratch_shapes=[
            pltpu.VMEM((depth, members * LANES), jnp.bfloat16),
            pltpu.VMEM((depth, members * LANES), jnp.bfloat16),
            pltpu.VMEM((out_rows, tile_cols + LANES), jnp.float32),
        ],
        compiler_params=params,
        name="rim",
    )(filter_taps, *tables, inner, to_core, to_cross, from_core, from_cross)


def solution(mesh):
    placed = (P(None, "narrow", "wide"), P(), P(), P(), P(), P(), P())
    return jax.shard_map(
        on_device,
        mesh=mesh,
        in_specs=placed,
        out_specs=(P("narrow", "wide"), P("narrow", "wide")),
        check_vma=False,
    )
```

```python
import functools

import jax
import jax.numpy as jnp
from jax import lax
from jax.experimental import pallas as pl
from jax.experimental.pallas import tpu as pltpu
from jax.sharding import PartitionSpec as P

LANES = 128
VMEM_BYTES = 48 << 20


def rounded(value, unit):
    return -(-value // unit) * unit


def sizes(tile_rows, side):
    half = side // 2
    out_rows = rounded(tile_rows + 2 * half, 8)
    in_rows = rounded(tile_rows + 4 * half, 16)
    return half, out_rows, in_rows


UPPER = 24
PART = 48


def band_matrix(half, begin, base, band_ref):
    kernel_total, wide = len(base), base[0].shape[1]
    rows, depth = band_ref.shape
    place = lax.rem(lax.broadcasted_iota(jnp.int32, (8, wide), 1), PART)
    lead = begin - 2 * half
    parts = []
    for kernel in range(kernel_total):
        spread = jnp.broadcast_to(base[kernel], (8, wide))
        block = pltpu.roll(spread, 0, 1, stride=1, stride_axis=0)
        for first in range(0, rows // kernel_total, 8):
            shift = first + lead
            plain = pltpu.roll(block, shift % wide, 1)
            wrapped = pltpu.roll(block, (shift + (PART if lead < 0 else -PART)) % wide, 1)
            if lead < 0:
                parts.append(jnp.where(place < PART + lead - 4, plain, wrapped))
            else:
                parts.append(jnp.where(place < lead, wrapped, plain))
    band_ref[...] = jnp.concatenate(parts, axis=0).astype(jnp.bfloat16)[:, :depth]


def factors_kernel(
    tile_rows, band_rows, half, coef_ref, weight_ref, start_ref, count_ref, after_ref, factor_ref
):
    kernel_total, members = coef_ref.shape[:2]
    out_rows = factor_ref.shape[1]
    place = lax.broadcasted_iota(jnp.int32, (out_rows, LANES), 0)
    row = lax.axis_index("narrow") * tile_rows - half + place
    y_coord = (2 * row + 1).astype(jnp.float32) / band_rows - 1.0
    weighting = []
    for member in range(members):
        inside = (row >= start_ref[member]) & (row < start_ref[member] + count_ref[member])
        weighting.append(jnp.where(inside, weight_ref[member], 0.0))
    denominator = functools.reduce(jnp.add, weighting)
    valid = (row >= 0) & (row < band_rows)
    inverse = jnp.where(valid, 1.0 / jnp.where(valid, denominator, 1.0), 0.0)
    for member in range(members):
        scale = weighting[member] * inverse
        for kernel in range(kernel_total):
            coeffs = [coef_ref[kernel, member, order] for order in range(6)]
            constant = coeffs[0] + coeffs[2] * y_coord + coeffs[5] * (y_coord * y_coord)
            index = 3 * (member * kernel_total + kernel)
            factor_ref[index] = constant * scale
            factor_ref[index + 1] = (coeffs[1] + coeffs[4] * y_coord) * scale
            factor_ref[index + 2] = coeffs[3] * scale


def spread_taps(basis_ref, square):
    kernel_total, side = basis_ref.shape[:2]
    rows = square.shape[0] // kernel_total
    wide = rounded(side * PART, LANES)
    square[...] = jnp.zeros_like(square)
    for kernel in range(kernel_total):
        square[kernel * rows : kernel * rows + side, :side] = basis_ref[kernel].astype(jnp.float32)
    across = lax.broadcasted_iota(jnp.int32, (LANES, wide), 0)
    begin = across * PART
    lane = lax.broadcasted_iota(jnp.int32, (LANES, wide), 1)
    onehot = jnp.where((lane >= begin) & (lane < begin + PART), 1.0, 0.0).astype(jnp.bfloat16)
    repeated = jnp.dot(
        square[...].astype(jnp.bfloat16), onehot, preferred_element_type=jnp.float32
    )
    down = lax.broadcasted_iota(jnp.int32, (rows, wide), 0)
    chosen = lax.rem(lax.broadcasted_iota(jnp.int32, (rows, wide), 1), PART) == down
    return [
        jnp.sum(
            jnp.where(chosen, repeated[kernel * rows : (kernel + 1) * rows], 0.0),
            axis=0,
            keepdims=True,
        )
        for kernel in range(kernel_total)
    ]


def bands_kernel(half, basis_ref, upper_ref, lower_ref, square):
    base = spread_taps(basis_ref, square)
    band_matrix(half, 0, base, upper_ref)
    band_matrix(half, UPPER, base, lower_ref)


def prepared(basis_kernels, poly_coef, weight, start, count, tile_rows):
    kernel_total, side = basis_kernels.shape[:2]
    members = poly_coef.shape[0]
    half, out_rows, _ = sizes(tile_rows, side)
    depth = side * PART
    smem = pl.BlockSpec(memory_space=pltpu.SMEM)
    vmem = pl.BlockSpec(memory_space=pltpu.VMEM)
    params = pltpu.CompilerParams(vmem_limit_bytes=VMEM_BYTES)
    band_rows = lax.axis_size("narrow") * tile_rows
    upper, lower = pl.pallas_call(
        functools.partial(bands_kernel, half),
        out_shape=(
            jax.ShapeDtypeStruct((kernel_total * UPPER, depth), jnp.bfloat16),
            jax.ShapeDtypeStruct((kernel_total * (out_rows - UPPER), depth), jnp.bfloat16),
        ),
        in_specs=[vmem],
        out_specs=(vmem, vmem),
        scratch_shapes=[pltpu.VMEM((kernel_total * rounded(side, 8), LANES), jnp.float32)],
        compiler_params=params,
        cost_estimate=pl.CostEstimate(flops=10**9, bytes_accessed=10**6, transcendentals=0),
        name="bands",
    )(basis_kernels)
    factors = pl.pallas_call(
        functools.partial(factors_kernel, tile_rows, band_rows, half),
        out_shape=jax.ShapeDtypeStruct((3 * members * kernel_total, out_rows, LANES), jnp.float32),
        in_specs=[smem] * 4 + [pl.BlockSpec(memory_space=pl.ANY)],
        out_specs=vmem,
        compiler_params=params,
        cost_estimate=pl.CostEstimate(flops=10**8, bytes_accessed=10**6, transcendentals=0),
        name="factors",
    )(poly_coef.transpose(1, 0, 2), weight, start, count, upper)
    return factors, upper, lower


def part_rows_of(moved):
    first, second, below, mixed, above = [moved[row : row + 16] for row in range(0, 80, 16)]
    place = lax.broadcasted_iota(jnp.int32, first.shape, 0)
    return (
        (first, jnp.where(place < 8, second, mixed), above),
        (jnp.where(place < 4, mixed, first), second, below),
    )


def fill_patches(window, half, side, patch_refs, lanes):
    width = window.shape[1]
    for tap in range(side):
        moved = pltpu.roll(window, (half - tap) % width, 1)
        for patch_ref, rows in zip(patch_refs, part_rows_of(moved), strict=True):
            for index, piece in enumerate(rows):
                begin = tap * PART + 16 * index
                patch_ref[begin : begin + 16, lanes] = piece


def products(band_refs, patch_refs):
    return [
        jnp.dot(band_ref[...], patch_ref[...], preferred_element_type=jnp.float32)
        for band_ref, patch_ref in zip(band_refs, patch_refs, strict=True)
    ]


def response_of(parts, kernel, kernel_total, lanes):
    pieces = []
    for part in parts:
        rows = part.shape[0] // kernel_total
        pieces.append(part[kernel * rows : (kernel + 1) * rows, lanes])
    return jnp.concatenate(pieces, axis=0)


def place_kernel(sent, start_ref, count_ref, *refs):
    peers = len(sent)
    tiles = refs[:peers][::-1]
    window_ref, core_ref, cross_ref, frame = refs[peers:]
    members, window_rows, tile_cols = window_ref.shape
    tile_rows = tiles[0].shape[1]
    narrow = lax.axis_index("narrow")
    odd = lax.rem(lax.axis_index("wide"), 2) == 1
    for index in range(peers):
        frame[jnp.bitwise_xor(narrow, index), sent[index] :] = tiles[index][...]
    lane = lax.broadcasted_iota(jnp.int32, (window_rows, LANES), 1)
    upper = lax.broadcasted_iota(jnp.int32, (16, tile_cols), 0) < 8
    leftward = jnp.zeros((window_rows, LANES), jnp.bfloat16)
    rightward = jnp.zeros((window_rows, LANES), jnp.bfloat16)
    for member in range(members):
        slot = narrow - start_ref[member] // tile_rows
        here = jnp.clip(slot, 0, peers - 1)
        above = jnp.clip(slot - 1, 0, peers - 1)
        below = jnp.clip(slot + 1, 0, peers - 1)
        window = jnp.concatenate(
            [
                frame[here, member],
                frame[below, member, :16],
                jnp.where(upper, frame[below, member, 16:], frame[above, member, :16]),
                frame[above, member, 16:],
            ]
        )
        place = lax.broadcasted_iota(jnp.int32, window.shape, 0)
        offset = jnp.where(place < window_rows - 24, place, place - window_rows)
        frame_row = offset + slot * tile_rows
        present = (frame_row >= 0) & (frame_row < count_ref[member])
        window = jnp.where(present, window, jnp.zeros((), window.dtype))
        window_ref[member] = window
        own = lane // 32 == member
        first = pltpu.roll(window[:, :LANES], 32 * member, 1)
        last = pltpu.roll(window[:, tile_cols - LANES :], (32 * member + 32) % LANES, 1)
        leftward = jnp.where(own, first, leftward)
        rightward = jnp.where(own, last, rightward)

    @pl.when(odd)
    def _():
        core_ref[...] = leftward
        cross_ref[...] = rightward

    @pl.when(jnp.logical_not(odd))
    def _():
        core_ref[...] = rightward
        cross_ref[...] = leftward


def column_position(column, band_cols):
    return (2 * column + 1).astype(jnp.float32) / band_cols - 1.0


def main_kernel(
    wide_peers,
    side,
    tile_rows,
    factor_ref,
    upper_ref,
    lower_ref,
    window_ref,
    out_ref,
    upper_patches,
    lower_patches,
):
    members, in_rows, tile_cols = window_ref.shape
    half, out_rows, _ = sizes(tile_rows, side)
    kernel_total = upper_ref.shape[0] // UPPER
    sums = [jnp.zeros((out_rows, tile_cols), jnp.float32) for _ in range(3)]
    group = upper_patches.shape[2] // tile_cols
    for begin in range(0, members, group):
        patch_refs = upper_patches.at[begin // group], lower_patches.at[begin // group]
        strips = [slice(index * tile_cols, (index + 1) * tile_cols) for index in range(group)]
        for index, lanes in enumerate(strips):
            fill_patches(window_ref[begin + index], half, side, patch_refs, lanes)
        parts = products((upper_ref, lower_ref), patch_refs)
        for index, lanes in enumerate(strips):
            for kernel in range(kernel_total):
                own = response_of(parts, kernel, kernel_total, lanes)
                place = 3 * ((begin + index) * kernel_total + kernel)
                for order in range(3):
                    factor = [factor_ref[place + order]] * (tile_cols // LANES)
                    sums[order] = sums[order] + jnp.concatenate(factor, axis=1) * own
    column = lax.axis_index("wide") * tile_cols + lax.broadcasted_iota(
        jnp.int32, (8, tile_cols), 1
    )
    x_coord = column_position(column, wide_peers * tile_cols)[:1]
    out_ref[...] = sums[0] + x_coord * (sums[1] + x_coord * sums[2])


def rim_kernel(
    wide_peers,
    side,
    members,
    taps_ref,
    factor_ref,
    upper_ref,
    lower_ref,
    inner_ref,
    to_core_ref,
    to_cross_ref,
    from_core_ref,
    from_cross_ref,
    coadd_ref,
    detection_ref,
    upper_patches,
    lower_patches,
    tall,
):
    tile_rows, tile_cols = coadd_ref.shape
    in_rows = to_core_ref.shape[0]
    half, out_rows, _ = sizes(tile_rows, side)
    rim = 2 * half
    kernel_total = upper_ref.shape[0] // UPPER
    band_cols = wide_peers * tile_cols
    wide = lax.axis_index("wide")
    odd = lax.rem(wide, 2) == 1

    none = jnp.zeros((in_rows, LANES), jnp.bfloat16)
    core, cross = from_core_ref[...], from_cross_ref[...]
    before = jnp.where(wide > 0, jnp.where(odd, core, cross), none)
    after = jnp.where(wide < wide_peers - 1, jnp.where(odd, cross, core), none)
    first = jnp.where(odd, to_core_ref[...], to_cross_ref[...])
    last = jnp.where(odd, to_cross_ref[...], to_core_ref[...])
    lane = lax.broadcasted_iota(jnp.int32, (in_rows, LANES), 1)
    zones = []
    for member in range(members):
        pieces = [
            pltpu.roll(piece, (target - 32 * member) % LANES, 1)
            for piece, target in ((before, -12), (first, rim), (last, 2 * rim - 12), (after, 3 * rim))
        ]
        zone = none
        for index in reversed(range(4)):
            zone = jnp.where(lane < (index + 1) * rim, pieces[index], zone)
        zones.append(zone)
    zones = jnp.concatenate(zones, axis=1)
    patch_refs = upper_patches, lower_patches
    fill_patches(zones, half, side, patch_refs, slice(0, members * LANES))
    parts = products((upper_ref, lower_ref), patch_refs)
    sums = [jnp.zeros((out_rows, LANES), jnp.float32) for _ in range(3)]
    for member in range(members):
        for kernel in range(kernel_total):
            lanes = slice(member * LANES, (member + 1) * LANES)
            own = response_of(parts, kernel, kernel_total, lanes)
            place = 3 * (member * kernel_total + kernel)
            for order in range(3):
                sums[order] = sums[order] + factor_ref[place + order] * own
    lane = lax.broadcasted_iota(jnp.int32, (out_rows, LANES), 1)
    column = wide * tile_cols + jnp.where(lane < 2 * rim, lane - rim, tile_cols - 3 * rim + lane)
    x_coord = column_position(column, band_cols)
    border = sums[0] + x_coord * (sums[1] + x_coord * sums[2])
    border = jnp.where((column >= 0) & (column < band_cols), border, 0.0)

    width = tile_cols + LANES
    head = pltpu.roll(border, LANES - rim, 1)
    tail = pltpu.roll(border, LANES - 3 * rim, 1)
    left = pltpu.roll(border, LANES - rim, 1)
    right = pltpu.roll(border, LANES - 3 * rim, 1)
    tall[:, :LANES] = jnp.where(lane < half, head, inner_ref[:, :LANES])
    tall[:, LANES : tile_cols - LANES] = inner_ref[:, LANES : tile_cols - LANES]
    tall[:, tile_cols - LANES : tile_cols] = jnp.where(
        lane >= LANES - half, tail, inner_ref[:, tile_cols - LANES :]
    )
    tall[:, tile_cols:] = jnp.where(lane < LANES // 2, right, left)
    coadd_ref[...] = tall[half : half + tile_rows, :tile_cols]
    filtered = taps_ref[0] * tall[:tile_rows, :]
    for tap in range(1, side):
        filtered = filtered + taps_ref[tap] * tall[tap : tap + tile_rows, :]
    detection = taps_ref[0] * pltpu.roll(filtered, half, 1)
    for tap in range(1, side):
        detection = detection + taps_ref[tap] * pltpu.roll(filtered, (half - tap) % width, 1)
    detection_ref[...] = detection[:, :tile_cols]


def on_device(
    exposures, basis_kernels, poly_coef, exposure_weight, row_start, row_count, filter_taps
):
    members, tile_rows, tile_cols = exposures.shape
    side = basis_kernels.shape[1]
    half, out_rows, in_rows = sizes(tile_rows, side)
    peers, wide_peers = lax.axis_size("narrow"), lax.axis_size("wide")
    smem = pl.BlockSpec(memory_space=pltpu.SMEM)
    vmem = pl.BlockSpec(memory_space=pltpu.VMEM)
    params = pltpu.CompilerParams(vmem_limit_bytes=VMEM_BYTES)

    def skipped(index):
        return 0 if any(abs(i - (i ^ index)) <= 1 for i in range(peers)) else 1

    sent = [skipped(index) for index in range(peers)]
    tiles = [exposures] * peers
    moving, latter = lax.optimization_barrier((exposures, exposures[1:]))
    for index in reversed(range(1, peers)):
        pairs = [(i, i ^ index) for i in range(peers)]
        whole = moving if index == 1 else exposures
        tiles[index] = lax.ppermute(latter if sent[index] else whole, "narrow", pairs)
    tables = prepared(
        basis_kernels, poly_coef, exposure_weight, row_start, row_count, tile_rows
    )
    depth = side * PART
    edge_shape = jax.ShapeDtypeStruct((in_rows, LANES), exposures.dtype)
    window_shape = jax.ShapeDtypeStruct((members, in_rows, tile_cols), exposures.dtype)
    window, to_core, to_cross = pl.pallas_call(
        functools.partial(place_kernel, sent),
        out_shape=(window_shape, edge_shape, edge_shape),
        in_specs=[smem] * 2 + [vmem] * peers,
        out_specs=[vmem] * 3,
        scratch_shapes=[pltpu.VMEM((peers, members, tile_rows, tile_cols), jnp.bfloat16)],
        compiler_params=params,
        name="place",
    )(row_start, row_count, *reversed(tiles))
    core_pairs = [(i, i ^ 1) for i in range(wide_peers)]
    cross_pairs = []
    for row in range(peers):
        for column in range(wide_peers):
            other = ((column - 1) ^ 1) + 1
            if other in (-1, wide_peers):
                pair = (row ^ 1, column)
            else:
                pair = (row, other)
            cross_pairs.append((column * peers + row, pair[1] * peers + pair[0]))
    from_core = lax.ppermute(to_core, "wide", core_pairs)
    from_cross = lax.ppermute(to_cross, ("wide", "narrow"), cross_pairs)

    inner = pl.pallas_call(
        functools.partial(main_kernel, wide_peers, side, tile_rows),
        out_shape=jax.ShapeDtypeStruct((out_rows, tile_cols), jnp.float32),
        in_specs=[vmem] * 4,
        out_specs=vmem,
        scratch_shapes=[pltpu.VMEM((members // 2, depth, 2 * tile_cols), jnp.bfloat16)] * 2,
        compiler_params=params,
        cost_estimate=pl.CostEstimate(flops=2 * 10**9, bytes_accessed=10**6, transcendentals=0),
        name="main",
    )(*tables, window)
    out = jax.ShapeDtypeStruct((tile_rows, tile_cols), jnp.float32)
    return pl.pallas_call(
        functools.partial(rim_kernel, wide_peers, side, members),
        out_shape=(out, out),
        in_specs=[smem] + [vmem] * 8,
        out_specs=(vmem, vmem),
        scratch_shapes=[
            pltpu.VMEM((depth, members * LANES), jnp.bfloat16),
            pltpu.VMEM((depth, members * LANES), jnp.bfloat16),
            pltpu.VMEM((out_rows, tile_cols + LANES), jnp.float32),
        ],
        compiler_params=params,
        name="rim",
    )(filter_taps, *tables, inner, to_core, to_cross, from_core, from_cross)


def solution(mesh):
    placed = (P(None, "narrow", "wide"), P(), P(), P(), P(), P(), P())
    return jax.shard_map(
        on_device,
        mesh=mesh,
        in_specs=placed,
        out_specs=(P("narrow", "wide"), P("narrow", "wide")),
        check_vma=False,
    )
```

```python
import functools

import jax
import jax.numpy as jnp
from jax import lax
from jax.experimental import pallas as pl
from jax.experimental.pallas import tpu as pltpu
from jax.sharding import PartitionSpec as P

LANES = 128
VMEM_BYTES = 48 << 20


def rounded(value, unit):
    return -(-value // unit) * unit


def sizes(tile_rows, side):
    half = side // 2
    out_rows = rounded(tile_rows + 2 * half, 8)
    in_rows = rounded(tile_rows + 4 * half, 16)
    return half, out_rows, in_rows


UPPER = 24
PART = 48


def band_matrix(half, begin, base, band_ref):
    kernel_total, wide = len(base), base[0].shape[1]
    rows, depth = band_ref.shape
    place = lax.rem(lax.broadcasted_iota(jnp.int32, (8, wide), 1), PART)
    lead = begin - 2 * half
    parts = []
    for kernel in range(kernel_total):
        spread = jnp.broadcast_to(base[kernel], (8, wide))
        block = pltpu.roll(spread, 0, 1, stride=1, stride_axis=0)
        for first in range(0, rows // kernel_total, 8):
            shift = first + lead
            plain = pltpu.roll(block, shift % wide, 1)
            wrapped = pltpu.roll(block, (shift + (PART if lead < 0 else -PART)) % wide, 1)
            if lead < 0:
                parts.append(jnp.where(place < PART + lead - 4, plain, wrapped))
            else:
                parts.append(jnp.where(place < lead, wrapped, plain))
    band_ref[...] = jnp.concatenate(parts, axis=0).astype(jnp.bfloat16)[:, :depth]


def factors_kernel(
    tile_rows,
    band_rows,
    half,
    coef_ref,
    weight_ref,
    start_ref,
    count_ref,
    taps_ref,
    after_ref,
    factor_ref,
    spread_ref,
    span_ref,
):
    for tap in range(taps_ref.shape[0]):
        spread_ref[tap : tap + 1, :] = jnp.full((1, LANES), taps_ref[tap], jnp.float32)
    for member in range(start_ref.shape[0]):
        span_ref[member] = jnp.full((16, LANES), start_ref[member], jnp.int32)
        span_ref[start_ref.shape[0] + member] = jnp.full((16, LANES), count_ref[member], jnp.int32)

    kernel_total, members = coef_ref.shape[:2]
    out_rows = factor_ref.shape[1]
    place = lax.broadcasted_iota(jnp.int32, (out_rows, LANES), 0)
    row = lax.axis_index("narrow") * tile_rows - half + place
    y_coord = (2 * row + 1).astype(jnp.float32) / band_rows - 1.0
    weighting = []
    for member in range(members):
        inside = (row >= start_ref[member]) & (row < start_ref[member] + count_ref[member])
        weighting.append(jnp.where(inside, weight_ref[member], 0.0))
    denominator = functools.reduce(jnp.add, weighting)
    valid = (row >= 0) & (row < band_rows)
    inverse = jnp.where(valid, 1.0 / jnp.where(valid, denominator, 1.0), 0.0)
    for member in range(members):
        scale = weighting[member] * inverse
        for kernel in range(kernel_total):
            coeffs = [coef_ref[kernel, member, order] for order in range(6)]
            constant = coeffs[0] + coeffs[2] * y_coord + coeffs[5] * (y_coord * y_coord)
            index = 3 * (member * kernel_total + kernel)
            factor_ref[index] = constant * scale
            factor_ref[index + 1] = (coeffs[1] + coeffs[4] * y_coord) * scale
            factor_ref[index + 2] = coeffs[3] * scale


def spread_taps(basis_ref, square):
    kernel_total, side = basis_ref.shape[:2]
    rows = square.shape[0] // kernel_total
    wide = rounded(side * PART, LANES)
    square[...] = jnp.zeros_like(square)
    for kernel in range(kernel_total):
        square[kernel * rows : kernel * rows + side, :side] = basis_ref[kernel].astype(jnp.float32)
    across = lax.broadcasted_iota(jnp.int32, (LANES, wide), 0)
    begin = across * PART
    lane = lax.broadcasted_iota(jnp.int32, (LANES, wide), 1)
    onehot = jnp.where((lane >= begin) & (lane < begin + PART), 1.0, 0.0).astype(jnp.bfloat16)
    repeated = jnp.dot(
        square[...].astype(jnp.bfloat16), onehot, preferred_element_type=jnp.float32
    )
    down = lax.broadcasted_iota(jnp.int32, (rows, wide), 0)
    chosen = lax.rem(lax.broadcasted_iota(jnp.int32, (rows, wide), 1), PART) == down
    return [
        jnp.sum(
            jnp.where(chosen, repeated[kernel * rows : (kernel + 1) * rows], 0.0),
            axis=0,
            keepdims=True,
        )
        for kernel in range(kernel_total)
    ]


def bands_kernel(half, basis_ref, upper_ref, lower_ref, square):
    base = spread_taps(basis_ref, square)
    band_matrix(half, 0, base, upper_ref)
    band_matrix(half, UPPER, base, lower_ref)


def prepared(basis_kernels, poly_coef, weight, start, count, taps, tile_rows):
    kernel_total, side = basis_kernels.shape[:2]
    members = poly_coef.shape[0]
    half, out_rows, _ = sizes(tile_rows, side)
    depth = side * PART
    smem = pl.BlockSpec(memory_space=pltpu.SMEM)
    vmem = pl.BlockSpec(memory_space=pltpu.VMEM)
    params = pltpu.CompilerParams(vmem_limit_bytes=VMEM_BYTES)
    band_rows = lax.axis_size("narrow") * tile_rows
    upper, lower = pl.pallas_call(
        functools.partial(bands_kernel, half),
        out_shape=(
            jax.ShapeDtypeStruct((kernel_total * UPPER, depth), jnp.bfloat16),
            jax.ShapeDtypeStruct((kernel_total * (out_rows - UPPER), depth), jnp.bfloat16),
        ),
        in_specs=[vmem],
        out_specs=(vmem, vmem),
        scratch_shapes=[pltpu.VMEM((kernel_total * rounded(side, 8), LANES), jnp.float32)],
        compiler_params=params,
        cost_estimate=pl.CostEstimate(flops=10**9, bytes_accessed=10**6, transcendentals=0),
        name="bands",
    )(basis_kernels)
    factors, spread, span = pl.pallas_call(
        functools.partial(factors_kernel, tile_rows, band_rows, half),
        out_shape=(
            jax.ShapeDtypeStruct((3 * members * kernel_total, out_rows, LANES), jnp.float32),
            jax.ShapeDtypeStruct((side, LANES), jnp.float32),
            jax.ShapeDtypeStruct((2 * members, 16, LANES), jnp.int32),
        ),
        in_specs=[smem] * 5 + [pl.BlockSpec(memory_space=pl.ANY)],
        out_specs=(vmem, vmem, vmem),
        compiler_params=params,
        cost_estimate=pl.CostEstimate(flops=10**8, bytes_accessed=10**6, transcendentals=0),
        name="factors",
    )(poly_coef.transpose(1, 0, 2), weight, start, count, taps, upper)
    return spread, span, (factors, upper, lower)


def part_rows_of(moved):
    first, second, below, mixed, above = [moved[row : row + 16] for row in range(0, 80, 16)]
    place = lax.broadcasted_iota(jnp.int32, first.shape, 0)
    return (
        (first, jnp.where(place < 8, second, mixed), above),
        (jnp.where(place < 4, mixed, first), second, below),
    )


def fill_patches(window, half, side, patch_refs, lanes):
    width = window.shape[1]
    for tap in range(side):
        moved = pltpu.roll(window, (half - tap) % width, 1)
        for patch_ref, rows in zip(patch_refs, part_rows_of(moved), strict=True):
            for index, piece in enumerate(rows):
                begin = tap * PART + 16 * index
                patch_ref[begin : begin + 16, lanes] = piece


def products(band_refs, patch_refs):
    results = []
    for band_ref, patch_ref in zip(band_refs, patch_refs, strict=True):
        depth = band_ref.shape[1]
        pieces = []
        for begin in range(0, depth, 256):
            end = min(begin + 256, depth)
            pieces.append(
                jnp.dot(
                    band_ref[:, begin:end],
                    patch_ref[begin:end, :],
                    preferred_element_type=jnp.float32,
                )
            )
        results.append(functools.reduce(jnp.add, pieces))
    return results


def response_of(parts, kernel, kernel_total, lanes):
    pieces = []
    for part in parts:
        rows = part.shape[0] // kernel_total
        pieces.append(part[kernel * rows : (kernel + 1) * rows, lanes])
    return jnp.concatenate(pieces, axis=0)


def place_kernel(sent, span_ref, *refs):
    peers = len(sent)
    tiles = refs[:peers][::-1]
    window_ref, core_ref, cross_ref = refs[peers:]
    members, window_rows, tile_cols = window_ref.shape
    tile_rows = tiles[0].shape[1]
    narrow = lax.axis_index("narrow")
    odd = lax.rem(lax.axis_index("wide"), 2) == 1
    lane = lax.broadcasted_iota(jnp.int32, (window_rows, LANES), 1)
    place = lax.broadcasted_iota(jnp.int32, (16, tile_cols), 0)
    leftward = jnp.zeros((window_rows, LANES), jnp.bfloat16)
    rightward = jnp.zeros((window_rows, LANES), jnp.bfloat16)
    none = jnp.zeros((16, tile_cols), jnp.bfloat16)

    def over_columns(array):
        return jnp.concatenate([array] * (tile_cols // LANES), axis=1)

    for member in range(members):
        lead = over_columns(narrow * tile_rows - span_ref[member])
        count = over_columns(span_ref[members + member])
        here, below, above = [none] * 2, [none] * 2, [none] * 2
        for index in range(peers):
            if member < sent[index]:
                continue
            tile = [tiles[index][member - sent[index], row : row + 16] for row in (0, 16)]
            base = jnp.bitwise_xor(narrow, index) * tile_rows
            for parts, offset in ((here, 0), (below, tile_rows), (above, -tile_rows)):
                chosen = lead + offset == base
                for part in range(2):
                    parts[part] = jnp.where(chosen, tile[part], parts[part])
        upper = place < 8
        groups = (
            (here[0], place),
            (here[1], place + 16),
            (below[0], place + tile_rows),
            (
                jnp.where(upper, below[1], above[0]),
                place + jnp.where(upper, tile_rows + 16, -tile_rows),
            ),
            (above[1], place - 16),
        )
        kept = []
        for values, offset in groups:
            frame_row = lead + offset
            kept.append(jnp.where((frame_row >= 0) & (frame_row < count), values, none))
        window = jnp.concatenate(kept, axis=0)
        window_ref[member] = window
        own = lane // 32 == member
        first = pltpu.roll(window[:, :LANES], 32 * member, 1)
        last = pltpu.roll(window[:, tile_cols - LANES :], (32 * member + 32) % LANES, 1)
        leftward = jnp.where(own, first, leftward)
        rightward = jnp.where(own, last, rightward)

    @pl.when(odd)
    def _():
        core_ref[...] = leftward
        cross_ref[...] = rightward

    @pl.when(jnp.logical_not(odd))
    def _():
        core_ref[...] = rightward
        cross_ref[...] = leftward


def column_position(column, band_cols):
    return (2 * column + 1).astype(jnp.float32) / band_cols - 1.0


def main_kernel(
    wide_peers,
    side,
    tile_rows,
    factor_ref,
    upper_ref,
    lower_ref,
    window_ref,
    out_ref,
    upper_patches,
    lower_patches,
):
    members, in_rows, tile_cols = window_ref.shape
    half, out_rows, _ = sizes(tile_rows, side)
    kernel_total = upper_ref.shape[0] // UPPER
    sums = [jnp.zeros((out_rows, tile_cols), jnp.float32) for _ in range(3)]
    group = upper_patches.shape[2] // tile_cols
    for begin in range(0, members, group):
        patch_refs = upper_patches.at[begin // group], lower_patches.at[begin // group]
        strips = [slice(index * tile_cols, (index + 1) * tile_cols) for index in range(group)]
        for index, lanes in enumerate(strips):
            fill_patches(window_ref[begin + index], half, side, patch_refs, lanes)
        parts = products((upper_ref, lower_ref), patch_refs)
        for index, lanes in enumerate(strips):
            for kernel in range(kernel_total):
                own = response_of(parts, kernel, kernel_total, lanes)
                place = 3 * ((begin + index) * kernel_total + kernel)
                for order in range(3):
                    factor = [factor_ref[place + order]] * (tile_cols // LANES)
                    sums[order] = sums[order] + jnp.concatenate(factor, axis=1) * own
    column = lax.axis_index("wide") * tile_cols + lax.broadcasted_iota(
        jnp.int32, (8, tile_cols), 1
    )
    x_coord = column_position(column, wide_peers * tile_cols)[:1]
    out_ref[...] = sums[0] + x_coord * (sums[1] + x_coord * sums[2])


def rim_kernel(
    wide_peers,
    side,
    members,
    taps_ref,
    factor_ref,
    upper_ref,
    lower_ref,
    inner_ref,
    to_core_ref,
    to_cross_ref,
    from_core_ref,
    from_cross_ref,
    coadd_ref,
    detection_ref,
    upper_patches,
    lower_patches,
    tall,
):
    tile_rows, tile_cols = coadd_ref.shape
    in_rows = to_core_ref.shape[0]
    half, out_rows, _ = sizes(tile_rows, side)
    rim = 2 * half
    kernel_total = upper_ref.shape[0] // UPPER
    band_cols = wide_peers * tile_cols
    wide = lax.axis_index("wide")
    odd = lax.rem(wide, 2) == 1

    none = jnp.zeros((in_rows, LANES), jnp.bfloat16)
    core, cross = from_core_ref[...], from_cross_ref[...]
    before = jnp.where(wide > 0, jnp.where(odd, core, cross), none)
    after = jnp.where(wide < wide_peers - 1, jnp.where(odd, cross, core), none)
    first = jnp.where(odd, to_core_ref[...], to_cross_ref[...])
    last = jnp.where(odd, to_cross_ref[...], to_core_ref[...])
    lane = lax.broadcasted_iota(jnp.int32, (in_rows, LANES), 1)
    zones = []
    for member in range(members):
        pieces = [
            pltpu.roll(piece, (target - 32 * member) % LANES, 1)
            for piece, target in ((before, -12), (first, rim), (last, 2 * rim - 12), (after, 3 * rim))
        ]
        zone = none
        for index in reversed(range(4)):
            zone = jnp.where(lane < (index + 1) * rim, pieces[index], zone)
        zones.append(zone)
    zones = jnp.concatenate(zones, axis=1)
    patch_refs = upper_patches, lower_patches
    fill_patches(zones, half, side, patch_refs, slice(0, members * LANES))
    parts = products((upper_ref, lower_ref), patch_refs)
    sums = [jnp.zeros((out_rows, LANES), jnp.float32) for _ in range(3)]
    for member in range(members):
        for kernel in range(kernel_total):
            lanes = slice(member * LANES, (member + 1) * LANES)
            own = response_of(parts, kernel, kernel_total, lanes)
            place = 3 * (member * kernel_total + kernel)
            for order in range(3):
                sums[order] = sums[order] + factor_ref[place + order] * own
    lane = lax.broadcasted_iota(jnp.int32, (out_rows, LANES), 1)
    column = wide * tile_cols + jnp.where(lane < 2 * rim, lane - rim, tile_cols - 3 * rim + lane)
    x_coord = column_position(column, band_cols)
    border = sums[0] + x_coord * (sums[1] + x_coord * sums[2])
    border = jnp.where((column >= 0) & (column < band_cols), border, 0.0)

    width = tile_cols + LANES
    head = pltpu.roll(border, LANES - rim, 1)
    tail = pltpu.roll(border, LANES - 3 * rim, 1)
    left = pltpu.roll(border, LANES - rim, 1)
    right = pltpu.roll(border, LANES - 3 * rim, 1)
    tall[:, :LANES] = jnp.where(lane < half, head, inner_ref[:, :LANES])
    tall[:, LANES : tile_cols - LANES] = inner_ref[:, LANES : tile_cols - LANES]
    tall[:, tile_cols - LANES : tile_cols] = jnp.where(
        lane >= LANES - half, tail, inner_ref[:, tile_cols - LANES :]
    )
    tall[:, tile_cols:] = jnp.where(lane < LANES // 2, right, left)
    coadd_ref[...] = tall[half : half + tile_rows, :tile_cols]
    taps = [
        jnp.broadcast_to(
            jnp.concatenate([taps_ref[tap : tap + 1, :]] * (width // LANES), axis=1),
            (tile_rows, width),
        )
        for tap in range(side)
    ]
    filtered = taps[0] * tall[:tile_rows, :]
    for tap in range(1, side):
        filtered = filtered + taps[tap] * tall[tap : tap + tile_rows, :]
    detection = taps[0] * pltpu.roll(filtered, half, 1)
    for tap in range(1, side):
        detection = detection + taps[tap] * pltpu.roll(filtered, (half - tap) % width, 1)
    detection_ref[...] = detection[:, :tile_cols]


def on_device(
    exposures, basis_kernels, poly_coef, exposure_weight, row_start, row_count, filter_taps
):
    members, tile_rows, tile_cols = exposures.shape
    side = basis_kernels.shape[1]
    half, out_rows, in_rows = sizes(tile_rows, side)
    peers, wide_peers = lax.axis_size("narrow"), lax.axis_size("wide")
    vmem = pl.BlockSpec(memory_space=pltpu.VMEM)
    params = pltpu.CompilerParams(vmem_limit_bytes=VMEM_BYTES)

    def skipped(index):
        return 0 if any(abs(i - (i ^ index)) <= 1 for i in range(peers)) else 1

    sent = [skipped(index) for index in range(peers)]
    tiles = [exposures] * peers
    moving, latter = lax.optimization_barrier((exposures, exposures[1:]))
    for index in reversed(range(1, peers)):
        pairs = [(i, i ^ index) for i in range(peers)]
        whole = moving if index == 1 else exposures
        tiles[index] = lax.ppermute(latter if sent[index] else whole, "narrow", pairs)
    taps, span, tables = prepared(
        basis_kernels,
        poly_coef,
        exposure_weight,
        row_start,
        row_count,
        filter_taps,
        tile_rows,
    )
    depth = side * PART
    edge_shape = jax.ShapeDtypeStruct((in_rows, LANES), exposures.dtype)
    window_shape = jax.ShapeDtypeStruct((members, in_rows, tile_cols), exposures.dtype)
    window, to_core, to_cross = pl.pallas_call(
        functools.partial(place_kernel, sent),
        out_shape=(window_shape, edge_shape, edge_shape),
        in_specs=[vmem] * (1 + peers),
        out_specs=[vmem] * 3,
        compiler_params=params,
        name="place",
    )(span, *reversed(tiles))
    core_pairs = [(i, i ^ 1) for i in range(wide_peers)]
    cross_pairs = []
    for row in range(peers):
        for column in range(wide_peers):
            other = ((column - 1) ^ 1) + 1
            if other in (-1, wide_peers):
                pair = (row ^ 1, column)
            else:
                pair = (row, other)
            cross_pairs.append((column * peers + row, pair[1] * peers + pair[0]))
    from_core = lax.ppermute(to_core, "wide", core_pairs)
    from_cross = lax.ppermute(to_cross, ("wide", "narrow"), cross_pairs)

    inner = pl.pallas_call(
        functools.partial(main_kernel, wide_peers, side, tile_rows),
        out_shape=jax.ShapeDtypeStruct((out_rows, tile_cols), jnp.float32),
        in_specs=[vmem] * 4,
        out_specs=vmem,
        scratch_shapes=[pltpu.VMEM((members // 2, depth, 2 * tile_cols), jnp.bfloat16)] * 2,
        compiler_params=params,
        cost_estimate=pl.CostEstimate(flops=2 * 10**9, bytes_accessed=10**6, transcendentals=0),
        name="main",
    )(*tables, window)
    out = jax.ShapeDtypeStruct((tile_rows, tile_cols), jnp.float32)
    return pl.pallas_call(
        functools.partial(rim_kernel, wide_peers, side, members),
        out_shape=(out, out),
        in_specs=[vmem] * 9,
        out_specs=(vmem, vmem),
        scratch_shapes=[
            pltpu.VMEM((depth, members * LANES), jnp.bfloat16),
            pltpu.VMEM((depth, members * LANES), jnp.bfloat16),
            pltpu.VMEM((out_rows, tile_cols + LANES), jnp.float32),
        ],
        compiler_params=params,
        name="rim",
    )(taps, *tables, inner, to_core, to_cross, from_core, from_cross)


def solution(mesh):
    placed = (P(None, "narrow", "wide"), P(), P(), P(), P(), P(), P())
    return jax.shard_map(
        on_device,
        mesh=mesh,
        in_specs=placed,
        out_specs=(P("narrow", "wide"), P("narrow", "wide")),
        check_vma=False,
    )
```

```python
import functools

import jax
import jax.numpy as jnp
from jax import lax
from jax.experimental import pallas as pl
from jax.experimental.pallas import tpu as pltpu
from jax.sharding import PartitionSpec as P

LANES = 128
VMEM_BYTES = 48 << 20


def rounded(value, unit):
    return -(-value // unit) * unit


def sizes(tile_rows, side):
    half = side // 2
    out_rows = rounded(tile_rows + 2 * half, 8)
    in_rows = rounded(tile_rows + 4 * half, 16)
    return half, out_rows, in_rows


UPPER = 24
PART = 48


def band_matrix(half, begin, base, band_ref):
    kernel_total, wide = len(base), base[0].shape[1]
    rows, depth = band_ref.shape
    place = lax.rem(lax.broadcasted_iota(jnp.int32, (8, wide), 1), PART)
    lead = begin - 2 * half
    parts = []
    for kernel in range(kernel_total):
        spread = jnp.broadcast_to(base[kernel], (8, wide))
        block = pltpu.roll(spread, 0, 1, stride=1, stride_axis=0)
        for first in range(0, rows // kernel_total, 8):
            shift = first + lead
            plain = pltpu.roll(block, shift % wide, 1)
            wrapped = pltpu.roll(block, (shift + (PART if lead < 0 else -PART)) % wide, 1)
            if lead < 0:
                parts.append(jnp.where(place < PART + lead - 4, plain, wrapped))
            else:
                parts.append(jnp.where(place < lead, wrapped, plain))
    band_ref[...] = jnp.concatenate(parts, axis=0).astype(jnp.bfloat16)[:, :depth]


def factors_kernel(
    tile_rows,
    band_rows,
    half,
    coef_ref,
    weight_ref,
    start_ref,
    count_ref,
    taps_ref,
    after_ref,
    factor_ref,
    spread_ref,
    span_ref,
):
    for tap in range(taps_ref.shape[0]):
        spread_ref[tap : tap + 1, :] = jnp.full((1, LANES), taps_ref[tap], jnp.float32)
    for member in range(start_ref.shape[0]):
        span_ref[member] = jnp.full((16, LANES), start_ref[member], jnp.int32)
        span_ref[start_ref.shape[0] + member] = jnp.full((16, LANES), count_ref[member], jnp.int32)

    kernel_total, members = coef_ref.shape[:2]
    out_rows = factor_ref.shape[1]
    place = lax.broadcasted_iota(jnp.int32, (out_rows, LANES), 0)
    row = lax.axis_index("narrow") * tile_rows - half + place
    y_coord = (2 * row + 1).astype(jnp.float32) / band_rows - 1.0
    weighting = []
    for member in range(members):
        inside = (row >= start_ref[member]) & (row < start_ref[member] + count_ref[member])
        weighting.append(jnp.where(inside, weight_ref[member], 0.0))
    denominator = functools.reduce(jnp.add, weighting)
    valid = (row >= 0) & (row < band_rows)
    inverse = jnp.where(valid, 1.0 / jnp.where(valid, denominator, 1.0), 0.0)
    for member in range(members):
        scale = weighting[member] * inverse
        for kernel in range(kernel_total):
            coeffs = [coef_ref[kernel, member, order] for order in range(6)]
            constant = coeffs[0] + coeffs[2] * y_coord + coeffs[5] * (y_coord * y_coord)
            index = 3 * (member * kernel_total + kernel)
            factor_ref[index] = constant * scale
            factor_ref[index + 1] = (coeffs[1] + coeffs[4] * y_coord) * scale
            factor_ref[index + 2] = coeffs[3] * scale


def spread_taps(basis_ref, square):
    kernel_total, side = basis_ref.shape[:2]
    rows = square.shape[0] // kernel_total
    wide = rounded(side * PART, LANES)
    square[...] = jnp.zeros_like(square)
    for kernel in range(kernel_total):
        square[kernel * rows : kernel * rows + side, :side] = basis_ref[kernel].astype(jnp.float32)
    across = lax.broadcasted_iota(jnp.int32, (LANES, wide), 0)
    begin = across * PART
    lane = lax.broadcasted_iota(jnp.int32, (LANES, wide), 1)
    onehot = jnp.where((lane >= begin) & (lane < begin + PART), 1.0, 0.0).astype(jnp.bfloat16)
    repeated = jnp.dot(
        square[...].astype(jnp.bfloat16), onehot, preferred_element_type=jnp.float32
    )
    down = lax.broadcasted_iota(jnp.int32, (rows, wide), 0)
    chosen = lax.rem(lax.broadcasted_iota(jnp.int32, (rows, wide), 1), PART) == down
    return [
        jnp.sum(
            jnp.where(chosen, repeated[kernel * rows : (kernel + 1) * rows], 0.0),
            axis=0,
            keepdims=True,
        )
        for kernel in range(kernel_total)
    ]


def bands_kernel(half, basis_ref, upper_ref, lower_ref, square):
    base = spread_taps(basis_ref, square)
    band_matrix(half, 0, base, upper_ref)
    band_matrix(half, UPPER, base, lower_ref)


def prepared(basis_kernels, poly_coef, weight, start, count, taps, tile_rows):
    kernel_total, side = basis_kernels.shape[:2]
    members = poly_coef.shape[0]
    half, out_rows, _ = sizes(tile_rows, side)
    depth = side * PART
    smem = pl.BlockSpec(memory_space=pltpu.SMEM)
    vmem = pl.BlockSpec(memory_space=pltpu.VMEM)
    params = pltpu.CompilerParams(vmem_limit_bytes=VMEM_BYTES)
    band_rows = lax.axis_size("narrow") * tile_rows
    upper, lower = pl.pallas_call(
        functools.partial(bands_kernel, half),
        out_shape=(
            jax.ShapeDtypeStruct((kernel_total * UPPER, depth), jnp.bfloat16),
            jax.ShapeDtypeStruct((kernel_total * (out_rows - UPPER), depth), jnp.bfloat16),
        ),
        in_specs=[vmem],
        out_specs=(vmem, vmem),
        scratch_shapes=[pltpu.VMEM((kernel_total * rounded(side, 8), LANES), jnp.float32)],
        compiler_params=params,
        cost_estimate=pl.CostEstimate(flops=10**9, bytes_accessed=10**6, transcendentals=0),
        name="bands",
    )(basis_kernels)
    factors, spread, span = pl.pallas_call(
        functools.partial(factors_kernel, tile_rows, band_rows, half),
        out_shape=(
            jax.ShapeDtypeStruct((3 * members * kernel_total, out_rows, LANES), jnp.float32),
            jax.ShapeDtypeStruct((side, LANES), jnp.float32),
            jax.ShapeDtypeStruct((2 * members, 16, LANES), jnp.int32),
        ),
        in_specs=[smem] * 5 + [pl.BlockSpec(memory_space=pl.ANY)],
        out_specs=(vmem, vmem, vmem),
        compiler_params=params,
        cost_estimate=pl.CostEstimate(flops=10**8, bytes_accessed=10**6, transcendentals=0),
        name="factors",
    )(poly_coef.transpose(1, 0, 2), weight, start, count, taps, upper)
    return spread, span, (factors, upper, lower)


def part_rows_of(moved):
    first, second, below, mixed, above = [moved[row : row + 16] for row in range(0, 80, 16)]
    place = lax.broadcasted_iota(jnp.int32, first.shape, 0)
    return (
        (first, jnp.where(place < 8, second, mixed), above),
        (jnp.where(place < 4, mixed, first), second, below),
    )


def fill_patches(window, half, side, patch_refs, lanes):
    width = window.shape[1]
    for tap in range(side):
        moved = pltpu.roll(window, (half - tap) % width, 1)
        for patch_ref, rows in zip(patch_refs, part_rows_of(moved), strict=True):
            for index, piece in enumerate(rows):
                begin = tap * PART + 16 * index
                patch_ref[begin : begin + 16, lanes] = piece


def products(band_refs, patch_refs):
    results = []
    for band_ref, patch_ref in zip(band_refs, patch_refs, strict=True):
        depth = band_ref.shape[1]
        pieces = []
        for begin in range(0, depth, 256):
            end = min(begin + 256, depth)
            pieces.append(
                jnp.dot(
                    band_ref[:, begin:end],
                    patch_ref[begin:end, :],
                    preferred_element_type=jnp.float32,
                )
            )
        results.append(functools.reduce(jnp.add, pieces))
    return results


def response_of(parts, kernel, kernel_total, lanes):
    pieces = []
    for part in parts:
        rows = part.shape[0] // kernel_total
        pieces.append(part[kernel * rows : (kernel + 1) * rows, lanes])
    return jnp.concatenate(pieces, axis=0)


def place_kernel(sent, span_ref, *refs):
    peers = len(sent)
    tiles = refs[:peers][::-1]
    window_ref, core_ref, cross_ref = refs[peers:]
    members, window_rows, tile_cols = window_ref.shape
    tile_rows = tiles[0].shape[1]
    narrow = lax.axis_index("narrow")
    odd = lax.rem(lax.axis_index("wide"), 2) == 1
    lane = lax.broadcasted_iota(jnp.int32, (window_rows, LANES), 1)
    place = lax.broadcasted_iota(jnp.int32, (16, tile_cols), 0)
    leftward = jnp.zeros((window_rows, LANES), jnp.bfloat16)
    rightward = jnp.zeros((window_rows, LANES), jnp.bfloat16)
    none = jnp.zeros((16, tile_cols), jnp.bfloat16)

    def over_columns(array):
        return jnp.concatenate([array] * (tile_cols // LANES), axis=1)

    for member in range(members):
        lead = over_columns(narrow * tile_rows - span_ref[member])
        count = over_columns(span_ref[members + member])
        here, below, above = [none] * 2, [none] * 2, [none] * 2
        for index in range(peers):
            if member < sent[index]:
                continue
            tile = [tiles[index][member - sent[index], row : row + 16] for row in (0, 16)]
            base = jnp.bitwise_xor(narrow, index) * tile_rows
            for parts, offset in ((here, 0), (below, tile_rows), (above, -tile_rows)):
                chosen = lead + offset == base
                for part in range(2):
                    parts[part] = jnp.where(chosen, tile[part], parts[part])
        upper = place < 8
        groups = (
            (here[0], place),
            (here[1], place + 16),
            (below[0], place + tile_rows),
            (
                jnp.where(upper, below[1], above[0]),
                place + jnp.where(upper, tile_rows + 16, -tile_rows),
            ),
            (above[1], place - 16),
        )
        kept = []
        for values, offset in groups:
            frame_row = lead + offset
            kept.append(jnp.where((frame_row >= 0) & (frame_row < count), values, none))
        window = jnp.concatenate(kept, axis=0)
        window_ref[member] = window
        own = lane // 32 == member
        first = pltpu.roll(window[:, :LANES], 32 * member, 1)
        last = pltpu.roll(window[:, tile_cols - LANES :], (32 * member + 32) % LANES, 1)
        leftward = jnp.where(own, first, leftward)
        rightward = jnp.where(own, last, rightward)

    @pl.when(odd)
    def _():
        core_ref[...] = leftward
        cross_ref[...] = rightward

    @pl.when(jnp.logical_not(odd))
    def _():
        core_ref[...] = rightward
        cross_ref[...] = leftward


def column_position(column, band_cols):
    return (2 * column + 1).astype(jnp.float32) / band_cols - 1.0


def filtered(taps_ref, side, tall, tile_rows):
    half = side // 2
    width = tall.shape[1]
    taps = [
        jnp.broadcast_to(
            jnp.concatenate([taps_ref[tap : tap + 1, :]] * (width // LANES), axis=1),
            (tile_rows, width),
        )
        for tap in range(side)
    ]
    across = taps[0] * tall[:tile_rows, :]
    for tap in range(1, side):
        across = across + taps[tap] * tall[tap : tap + tile_rows, :]
    result = taps[0] * pltpu.roll(across, half, 1)
    for tap in range(1, side):
        result = result + taps[tap] * pltpu.roll(across, (half - tap) % width, 1)
    return result


def main_kernel(
    wide_peers,
    side,
    tile_rows,
    taps_ref,
    factor_ref,
    upper_ref,
    lower_ref,
    window_ref,
    out_ref,
    inner_detection_ref,
    upper_patches,
    lower_patches,
):
    members, in_rows, tile_cols = window_ref.shape
    half, out_rows, _ = sizes(tile_rows, side)
    kernel_total = upper_ref.shape[0] // UPPER
    sums = [jnp.zeros((out_rows, tile_cols), jnp.float32) for _ in range(3)]
    group = upper_patches.shape[2] // tile_cols
    for begin in range(0, members, group):
        patch_refs = upper_patches.at[begin // group], lower_patches.at[begin // group]
        strips = [slice(index * tile_cols, (index + 1) * tile_cols) for index in range(group)]
        for index, lanes in enumerate(strips):
            fill_patches(window_ref[begin + index], half, side, patch_refs, lanes)
        parts = products((upper_ref, lower_ref), patch_refs)
        for index, lanes in enumerate(strips):
            for kernel in range(kernel_total):
                own = response_of(parts, kernel, kernel_total, lanes)
                place = 3 * ((begin + index) * kernel_total + kernel)
                for order in range(3):
                    factor = [factor_ref[place + order]] * (tile_cols // LANES)
                    sums[order] = sums[order] + jnp.concatenate(factor, axis=1) * own
    column = lax.axis_index("wide") * tile_cols + lax.broadcasted_iota(
        jnp.int32, (8, tile_cols), 1
    )
    x_coord = column_position(column, wide_peers * tile_cols)[:1]
    out_ref[...] = sums[0] + x_coord * (sums[1] + x_coord * sums[2])
    inner_detection_ref[...] = filtered(taps_ref, side, out_ref, tile_rows)


def rim_kernel(
    wide_peers,
    side,
    members,
    taps_ref,
    factor_ref,
    upper_ref,
    lower_ref,
    inner_ref,
    inner_detection_ref,
    to_core_ref,
    to_cross_ref,
    from_core_ref,
    from_cross_ref,
    coadd_ref,
    detection_ref,
    upper_patches,
    lower_patches,
    tall,
):
    tile_rows, tile_cols = coadd_ref.shape
    in_rows = to_core_ref.shape[0]
    half, out_rows, _ = sizes(tile_rows, side)
    rim = 2 * half
    kernel_total = upper_ref.shape[0] // UPPER
    band_cols = wide_peers * tile_cols
    wide = lax.axis_index("wide")
    odd = lax.rem(wide, 2) == 1

    none = jnp.zeros((in_rows, LANES), jnp.bfloat16)
    core, cross = from_core_ref[...], from_cross_ref[...]
    before = jnp.where(wide > 0, jnp.where(odd, core, cross), none)
    after = jnp.where(wide < wide_peers - 1, jnp.where(odd, cross, core), none)
    first = jnp.where(odd, to_core_ref[...], to_cross_ref[...])
    last = jnp.where(odd, to_cross_ref[...], to_core_ref[...])
    lane = lax.broadcasted_iota(jnp.int32, (in_rows, LANES), 1)
    zones = []
    for member in range(members):
        pieces = [
            pltpu.roll(piece, (target - 32 * member) % LANES, 1)
            for piece, target in ((before, -12), (first, rim), (last, 2 * rim - 12), (after, 3 * rim))
        ]
        zone = none
        for index in reversed(range(4)):
            zone = jnp.where(lane < (index + 1) * rim, pieces[index], zone)
        zones.append(zone)
    zones = jnp.concatenate(zones, axis=1)
    patch_refs = upper_patches, lower_patches
    fill_patches(zones, half, side, patch_refs, slice(0, members * LANES))
    parts = products((upper_ref, lower_ref), patch_refs)
    sums = [jnp.zeros((out_rows, LANES), jnp.float32) for _ in range(3)]
    for member in range(members):
        for kernel in range(kernel_total):
            lanes = slice(member * LANES, (member + 1) * LANES)
            own = response_of(parts, kernel, kernel_total, lanes)
            place = 3 * (member * kernel_total + kernel)
            for order in range(3):
                sums[order] = sums[order] + factor_ref[place + order] * own
    lane = lax.broadcasted_iota(jnp.int32, (out_rows, LANES), 1)
    column = wide * tile_cols + jnp.where(lane < 2 * rim, lane - rim, tile_cols - 3 * rim + lane)
    x_coord = column_position(column, band_cols)
    border = sums[0] + x_coord * (sums[1] + x_coord * sums[2])
    border = jnp.where((column >= 0) & (column < band_cols), border, 0.0)

    middle = LANES // 2
    first_inner = inner_ref[:, :LANES]
    last_inner = inner_ref[:, tile_cols - LANES :]
    edge = jnp.where(
        lane < middle,
        jnp.where(lane < rim + half, border, pltpu.roll(first_inner, rim, 1)),
        jnp.where(
            lane >= LANES - rim - half,
            pltpu.roll(border, LANES - 4 * rim, 1),
            pltpu.roll(last_inner, LANES - rim, 1),
        ),
    )
    tall[...] = edge
    coadd_ref[...] = inner_ref[half : half + tile_rows, :]
    edge_detection = filtered(taps_ref, side, tall, tile_rows)
    edge_coadd = tall[half : half + tile_rows, :]
    detection_ref[...] = inner_detection_ref[...]
    lane = lane[:tile_rows]
    for out_ref, values, reach in (
        (coadd_ref, edge_coadd, half),
        (detection_ref, edge_detection, rim),
    ):
        head = pltpu.roll(values, LANES - rim, 1)
        tail = pltpu.roll(values, rim, 1)
        out_ref[:, :LANES] = jnp.where(lane < reach, head, out_ref[:, :LANES])
        out_ref[:, tile_cols - LANES :] = jnp.where(
            lane >= LANES - reach, tail, out_ref[:, tile_cols - LANES :]
        )


def on_device(
    exposures, basis_kernels, poly_coef, exposure_weight, row_start, row_count, filter_taps
):
    members, tile_rows, tile_cols = exposures.shape
    side = basis_kernels.shape[1]
    half, out_rows, in_rows = sizes(tile_rows, side)
    peers, wide_peers = lax.axis_size("narrow"), lax.axis_size("wide")
    vmem = pl.BlockSpec(memory_space=pltpu.VMEM)
    params = pltpu.CompilerParams(vmem_limit_bytes=VMEM_BYTES)

    def skipped(index):
        return 0 if any(abs(i - (i ^ index)) <= 1 for i in range(peers)) else 1

    sent = [skipped(index) for index in range(peers)]
    tiles = [exposures] * peers
    for index in reversed(range(1, peers)):
        pairs = [(i, i ^ index) for i in range(peers)]
        tiles[index] = lax.ppermute(exposures[sent[index] :], "narrow", pairs)
    taps, span, tables = prepared(
        basis_kernels,
        poly_coef,
        exposure_weight,
        row_start,
        row_count,
        filter_taps,
        tile_rows,
    )
    depth = side * PART
    edge_shape = jax.ShapeDtypeStruct((in_rows, LANES), exposures.dtype)
    window_shape = jax.ShapeDtypeStruct((members, in_rows, tile_cols), exposures.dtype)
    window, to_core, to_cross = pl.pallas_call(
        functools.partial(place_kernel, sent),
        out_shape=(window_shape, edge_shape, edge_shape),
        in_specs=[vmem] * (1 + peers),
        out_specs=[vmem] * 3,
        compiler_params=params,
        name="place",
    )(span, *reversed(tiles))
    core_pairs = [(i, i ^ 1) for i in range(wide_peers)]
    cross_pairs = []
    for row in range(peers):
        for column in range(wide_peers):
            other = ((column - 1) ^ 1) + 1
            if other in (-1, wide_peers):
                pair = (row ^ 1, column)
            else:
                pair = (row, other)
            cross_pairs.append((column * peers + row, pair[1] * peers + pair[0]))
    from_core = lax.ppermute(to_core, "wide", core_pairs)
    from_cross = lax.ppermute(to_cross, ("wide", "narrow"), cross_pairs)

    inner, inner_detection = pl.pallas_call(
        functools.partial(main_kernel, wide_peers, side, tile_rows),
        out_shape=(
            jax.ShapeDtypeStruct((out_rows, tile_cols), jnp.float32),
            jax.ShapeDtypeStruct((tile_rows, tile_cols), jnp.float32),
        ),
        in_specs=[vmem] * 5,
        out_specs=(vmem, vmem),
        scratch_shapes=[pltpu.VMEM((members // 2, depth, 2 * tile_cols), jnp.bfloat16)] * 2,
        compiler_params=params,
        cost_estimate=pl.CostEstimate(flops=2 * 10**9, bytes_accessed=10**6, transcendentals=0),
        name="main",
    )(taps, *tables, window)
    out = jax.ShapeDtypeStruct((tile_rows, tile_cols), jnp.float32)
    return pl.pallas_call(
        functools.partial(rim_kernel, wide_peers, side, members),
        out_shape=(out, out),
        in_specs=[vmem] * 10,
        out_specs=(vmem, vmem),
        scratch_shapes=[
            pltpu.VMEM((depth, members * LANES), jnp.bfloat16),
            pltpu.VMEM((depth, members * LANES), jnp.bfloat16),
            pltpu.VMEM((out_rows, LANES), jnp.float32),
        ],
        compiler_params=params,
        name="rim",
    )(taps, *tables, inner, inner_detection, to_core, to_cross, from_core, from_cross)


def solution(mesh):
    placed = (P(None, "narrow", "wide"), P(), P(), P(), P(), P(), P())
    return jax.shard_map(
        on_device,
        mesh=mesh,
        in_specs=placed,
        out_specs=(P("narrow", "wide"), P("narrow", "wide")),
        check_vma=False,
    )
```

```python
import functools

import jax
import jax.numpy as jnp
from jax import lax
from jax.experimental import pallas as pl
from jax.experimental.pallas import tpu as pltpu
from jax.sharding import PartitionSpec as P

LANES = 128
VMEM_BYTES = 48 << 20


def rounded(value, unit):
    return -(-value // unit) * unit


def sizes(tile_rows, side):
    half = side // 2
    out_rows = rounded(tile_rows + 2 * half, 8)
    in_rows = rounded(tile_rows + 4 * half, 16)
    return half, out_rows, in_rows


UPPER = 24
PART = 48


def band_matrix(half, begin, base, band_ref):
    kernel_total, wide = len(base), base[0].shape[1]
    rows, depth = band_ref.shape
    place = lax.rem(lax.broadcasted_iota(jnp.int32, (8, wide), 1), PART)
    lead = begin - 2 * half
    parts = []
    for kernel in range(kernel_total):
        spread = jnp.broadcast_to(base[kernel], (8, wide))
        block = pltpu.roll(spread, 0, 1, stride=1, stride_axis=0)
        for first in range(0, rows // kernel_total, 8):
            shift = first + lead
            plain = pltpu.roll(block, shift % wide, 1)
            wrapped = pltpu.roll(block, (shift + (PART if lead < 0 else -PART)) % wide, 1)
            if lead < 0:
                parts.append(jnp.where(place < PART + lead - 4, plain, wrapped))
            else:
                parts.append(jnp.where(place < lead, wrapped, plain))
    band_ref[...] = jnp.concatenate(parts, axis=0).astype(jnp.bfloat16)[:, :depth]


def factors_kernel(
    tile_rows,
    band_rows,
    half,
    coef_ref,
    weight_ref,
    start_ref,
    count_ref,
    taps_ref,
    after_ref,
    factor_ref,
    spread_ref,
    span_ref,
    rows_ref,
):
    wide = lax.broadcasted_iota(jnp.int32, (8, LANES), 1)
    line = jnp.zeros((8, LANES), jnp.float32)
    for tap in range(taps_ref.shape[0]):
        line = jnp.where(wide == tap, taps_ref[tap], line)
    tile = pltpu.roll(line, 0, 1, stride=1, stride_axis=0)
    grid = [pltpu.roll(tile, first, 1) for first in range(0, rows_ref.shape[0] // 2, 8)]
    grid = jnp.concatenate(grid, axis=0)
    high = grid.astype(jnp.bfloat16).astype(jnp.float32)
    both = high + pltpu.roll(high, LANES // 2, 1)
    rows_ref[...] = jnp.concatenate([both, grid - high], axis=0).astype(jnp.bfloat16)
    for tap in range(taps_ref.shape[0]):
        spread_ref[tap : tap + 1, :] = jnp.full((1, LANES), taps_ref[tap], jnp.float32)
    for member in range(start_ref.shape[0]):
        span_ref[member] = jnp.full((16, LANES), start_ref[member], jnp.int32)
        span_ref[start_ref.shape[0] + member] = jnp.full((16, LANES), count_ref[member], jnp.int32)

    kernel_total, members = coef_ref.shape[:2]
    out_rows = factor_ref.shape[1]
    place = lax.broadcasted_iota(jnp.int32, (out_rows, LANES), 0)
    row = lax.axis_index("narrow") * tile_rows - half + place
    y_coord = (2 * row + 1).astype(jnp.float32) / band_rows - 1.0
    weighting = []
    for member in range(members):
        inside = (row >= start_ref[member]) & (row < start_ref[member] + count_ref[member])
        weighting.append(jnp.where(inside, weight_ref[member], 0.0))
    denominator = functools.reduce(jnp.add, weighting)
    valid = (row >= 0) & (row < band_rows)
    inverse = jnp.where(valid, 1.0 / jnp.where(valid, denominator, 1.0), 0.0)
    for member in range(members):
        scale = weighting[member] * inverse
        for kernel in range(kernel_total):
            coeffs = [coef_ref[kernel, member, order] for order in range(6)]
            constant = coeffs[0] + coeffs[2] * y_coord + coeffs[5] * (y_coord * y_coord)
            index = 3 * (member * kernel_total + kernel)
            factor_ref[index] = constant * scale
            factor_ref[index + 1] = (coeffs[1] + coeffs[4] * y_coord) * scale
            factor_ref[index + 2] = coeffs[3] * scale


def spread_taps(basis_ref, square):
    kernel_total, side = basis_ref.shape[:2]
    rows = square.shape[0] // kernel_total
    wide = rounded(side * PART, LANES)
    square[...] = jnp.zeros_like(square)
    for kernel in range(kernel_total):
        square[kernel * rows : kernel * rows + side, :side] = basis_ref[kernel].astype(jnp.float32)
    across = lax.broadcasted_iota(jnp.int32, (LANES, wide), 0)
    begin = across * PART
    lane = lax.broadcasted_iota(jnp.int32, (LANES, wide), 1)
    onehot = jnp.where((lane >= begin) & (lane < begin + PART), 1.0, 0.0).astype(jnp.bfloat16)
    repeated = jnp.dot(
        square[...].astype(jnp.bfloat16), onehot, preferred_element_type=jnp.float32
    )
    down = lax.broadcasted_iota(jnp.int32, (rows, wide), 0)
    chosen = lax.rem(lax.broadcasted_iota(jnp.int32, (rows, wide), 1), PART) == down
    return [
        jnp.sum(
            jnp.where(chosen, repeated[kernel * rows : (kernel + 1) * rows], 0.0),
            axis=0,
            keepdims=True,
        )
        for kernel in range(kernel_total)
    ]


def bands_kernel(half, basis_ref, upper_ref, lower_ref, square):
    base = spread_taps(basis_ref, square)
    band_matrix(half, 0, base, upper_ref)
    band_matrix(half, UPPER, base, lower_ref)


def prepared(basis_kernels, poly_coef, weight, start, count, taps, tile_rows):
    kernel_total, side = basis_kernels.shape[:2]
    members = poly_coef.shape[0]
    half, out_rows, _ = sizes(tile_rows, side)
    depth = side * PART
    smem = pl.BlockSpec(memory_space=pltpu.SMEM)
    vmem = pl.BlockSpec(memory_space=pltpu.VMEM)
    params = pltpu.CompilerParams(vmem_limit_bytes=VMEM_BYTES)
    band_rows = lax.axis_size("narrow") * tile_rows
    upper, lower = pl.pallas_call(
        functools.partial(bands_kernel, half),
        out_shape=(
            jax.ShapeDtypeStruct((kernel_total * UPPER, depth), jnp.bfloat16),
            jax.ShapeDtypeStruct((kernel_total * (out_rows - UPPER), depth), jnp.bfloat16),
        ),
        in_specs=[vmem],
        out_specs=(vmem, vmem),
        scratch_shapes=[pltpu.VMEM((kernel_total * rounded(side, 8), LANES), jnp.float32)],
        compiler_params=params,
        cost_estimate=pl.CostEstimate(flops=10**9, bytes_accessed=10**6, transcendentals=0),
        name="bands",
    )(basis_kernels)
    factors, spread, span, rows = pl.pallas_call(
        functools.partial(factors_kernel, tile_rows, band_rows, half),
        out_shape=(
            jax.ShapeDtypeStruct((3 * members * kernel_total, out_rows, LANES), jnp.float32),
            jax.ShapeDtypeStruct((side, LANES), jnp.float32),
            jax.ShapeDtypeStruct((2 * members, 16, LANES), jnp.int32),
            jax.ShapeDtypeStruct((2 * tile_rows, LANES), jnp.bfloat16),
        ),
        in_specs=[smem] * 5 + [pl.BlockSpec(memory_space=pl.ANY)],
        out_specs=(vmem, vmem, vmem, vmem),
        compiler_params=params,
        cost_estimate=pl.CostEstimate(flops=10**8, bytes_accessed=10**6, transcendentals=0),
        name="factors",
    )(poly_coef.transpose(1, 0, 2), weight, start, count, taps, upper)
    return (spread, rows), span, (factors, upper, lower)


def part_rows_of(moved):
    first, second, below, mixed, above = [moved[row : row + 16] for row in range(0, 80, 16)]
    place = lax.broadcasted_iota(jnp.int32, first.shape, 0)
    return (
        (first, jnp.where(place < 8, second, mixed), above),
        (jnp.where(place < 4, mixed, first), second, below),
    )


def fill_patches(window, half, side, patch_refs, lanes):
    width = window.shape[1]
    for tap in range(side):
        moved = pltpu.roll(window, (half - tap) % width, 1)
        for patch_ref, rows in zip(patch_refs, part_rows_of(moved), strict=True):
            for index, piece in enumerate(rows):
                begin = tap * PART + 16 * index
                patch_ref[begin : begin + 16, lanes] = piece


def products(band_refs, patch_refs):
    results = []
    for band_ref, patch_ref in zip(band_refs, patch_refs, strict=True):
        depth = band_ref.shape[1]
        pieces = []
        for begin in range(0, depth, 256):
            end = min(begin + 256, depth)
            pieces.append(
                jnp.dot(
                    band_ref[:, begin:end],
                    patch_ref[begin:end, :],
                    preferred_element_type=jnp.float32,
                )
            )
        results.append(functools.reduce(jnp.add, pieces))
    return results


def response_of(parts, kernel, kernel_total, lanes):
    pieces = []
    for part in parts:
        rows = part.shape[0] // kernel_total
        pieces.append(part[kernel * rows : (kernel + 1) * rows, lanes])
    return jnp.concatenate(pieces, axis=0)


def place_kernel(sent, span_ref, *refs):
    peers = len(sent)
    tiles = refs[:peers][::-1]
    window_ref, core_ref, cross_ref = refs[peers:]
    members, window_rows, tile_cols = window_ref.shape
    tile_rows = tiles[0].shape[1]
    narrow = lax.axis_index("narrow")
    odd = lax.rem(lax.axis_index("wide"), 2) == 1
    lane = lax.broadcasted_iota(jnp.int32, (window_rows, LANES), 1)
    place = lax.broadcasted_iota(jnp.int32, (16, tile_cols), 0)
    leftward = jnp.zeros((window_rows, LANES), jnp.bfloat16)
    rightward = jnp.zeros((window_rows, LANES), jnp.bfloat16)
    none = jnp.zeros((16, tile_cols), jnp.bfloat16)

    def over_columns(array):
        return jnp.concatenate([array] * (tile_cols // LANES), axis=1)

    for member in range(members):
        lead = over_columns(narrow * tile_rows - span_ref[member])
        count = over_columns(span_ref[members + member])
        here, below, above = [none] * 2, [none] * 2, [none] * 2
        for index in range(peers):
            if member < sent[index]:
                continue
            tile = [tiles[index][member - sent[index], row : row + 16] for row in (0, 16)]
            base = jnp.bitwise_xor(narrow, index) * tile_rows
            for parts, offset in ((here, 0), (below, tile_rows), (above, -tile_rows)):
                chosen = lead + offset == base
                for part in range(2):
                    parts[part] = jnp.where(chosen, tile[part], parts[part])
        upper = place < 8
        groups = (
            (here[0], place),
            (here[1], place + 16),
            (below[0], place + tile_rows),
            (
                jnp.where(upper, below[1], above[0]),
                place + jnp.where(upper, tile_rows + 16, -tile_rows),
            ),
            (above[1], place - 16),
        )
        kept = []
        for values, offset in groups:
            frame_row = lead + offset
            kept.append(jnp.where((frame_row >= 0) & (frame_row < count), values, none))
        window = jnp.concatenate(kept, axis=0)
        window_ref[member] = window
        own = lane // 32 == member
        first = pltpu.roll(window[:, :LANES], 32 * member, 1)
        last = pltpu.roll(window[:, tile_cols - LANES :], (32 * member + 32) % LANES, 1)
        leftward = jnp.where(own, first, leftward)
        rightward = jnp.where(own, last, rightward)

    @pl.when(odd)
    def _():
        core_ref[...] = leftward
        cross_ref[...] = rightward

    @pl.when(jnp.logical_not(odd))
    def _():
        core_ref[...] = rightward
        cross_ref[...] = leftward


def column_position(column, band_cols):
    return (2 * column + 1).astype(jnp.float32) / band_cols - 1.0


def filtered(taps_ref, rows_ref, side, tall, tile_rows):
    half = side // 2
    width = tall.shape[1]
    taps = [
        jnp.broadcast_to(
            jnp.concatenate([taps_ref[tap : tap + 1, :]] * (width // LANES), axis=1),
            (tile_rows, width),
        )
        for tap in range(side)
    ]
    if rows_ref is None:
        across = taps[0] * tall[:tile_rows, :]
        for tap in range(1, side):
            across = across + taps[tap] * tall[tap : tap + tile_rows, :]
    else:
        coadded = jnp.concatenate(
            [tall, jnp.zeros((LANES // 2 - tall.shape[0], width), jnp.float32)], axis=0
        )
        high = coadded.astype(jnp.bfloat16)
        low = (coadded - high.astype(jnp.float32)).astype(jnp.bfloat16)
        split = jnp.concatenate([high, low], axis=0)
        across = jnp.dot(rows_ref[...], split, preferred_element_type=jnp.float32)
        across = across[:tile_rows] + across[tile_rows:]
    result = taps[0] * pltpu.roll(across, half, 1)
    for tap in range(1, side):
        result = result + taps[tap] * pltpu.roll(across, (half - tap) % width, 1)
    return result


def main_kernel(
    wide_peers,
    side,
    tile_rows,
    taps_ref,
    rows_ref,
    factor_ref,
    upper_ref,
    lower_ref,
    window_ref,
    out_ref,
    inner_detection_ref,
    upper_patches,
    lower_patches,
):
    members, in_rows, tile_cols = window_ref.shape
    half, out_rows, _ = sizes(tile_rows, side)
    kernel_total = upper_ref.shape[0] // UPPER
    sums = [jnp.zeros((out_rows, tile_cols), jnp.float32) for _ in range(3)]
    group = upper_patches.shape[2] // tile_cols
    for begin in range(0, members, group):
        patch_refs = upper_patches.at[begin // group], lower_patches.at[begin // group]
        strips = [slice(index * tile_cols, (index + 1) * tile_cols) for index in range(group)]
        for index, lanes in enumerate(strips):
            fill_patches(window_ref[begin + index], half, side, patch_refs, lanes)
        parts = products((upper_ref, lower_ref), patch_refs)
        for index, lanes in enumerate(strips):
            for kernel in range(kernel_total):
                own = response_of(parts, kernel, kernel_total, lanes)
                place = 3 * ((begin + index) * kernel_total + kernel)
                for order in range(3):
                    factor = [factor_ref[place + order]] * (tile_cols // LANES)
                    sums[order] = sums[order] + jnp.concatenate(factor, axis=1) * own
    column = lax.axis_index("wide") * tile_cols + lax.broadcasted_iota(
        jnp.int32, (8, tile_cols), 1
    )
    x_coord = column_position(column, wide_peers * tile_cols)[:1]
    coadded = sums[0] + x_coord * (sums[1] + x_coord * sums[2])
    out_ref[...] = coadded
    inner_detection_ref[...] = filtered(taps_ref, rows_ref, side, coadded, tile_rows)


def rim_kernel(
    wide_peers,
    side,
    members,
    taps_ref,
    factor_ref,
    upper_ref,
    lower_ref,
    inner_ref,
    inner_detection_ref,
    to_core_ref,
    to_cross_ref,
    from_core_ref,
    from_cross_ref,
    coadd_ref,
    detection_ref,
    upper_patches,
    lower_patches,
    tall,
):
    tile_rows, tile_cols = coadd_ref.shape
    in_rows = to_core_ref.shape[0]
    half, out_rows, _ = sizes(tile_rows, side)
    rim = 2 * half
    kernel_total = upper_ref.shape[0] // UPPER
    band_cols = wide_peers * tile_cols
    wide = lax.axis_index("wide")
    odd = lax.rem(wide, 2) == 1

    none = jnp.zeros((in_rows, LANES), jnp.bfloat16)
    core, cross = from_core_ref[...], from_cross_ref[...]
    before = jnp.where(wide > 0, jnp.where(odd, core, cross), none)
    after = jnp.where(wide < wide_peers - 1, jnp.where(odd, cross, core), none)
    first = jnp.where(odd, to_core_ref[...], to_cross_ref[...])
    last = jnp.where(odd, to_cross_ref[...], to_core_ref[...])
    lane = lax.broadcasted_iota(jnp.int32, (in_rows, LANES), 1)
    zones = []
    for member in range(members):
        pieces = [
            pltpu.roll(piece, (target - 32 * member) % LANES, 1)
            for piece, target in ((before, -12), (first, rim), (last, 2 * rim - 12), (after, 3 * rim))
        ]
        zone = none
        for index in reversed(range(4)):
            zone = jnp.where(lane < (index + 1) * rim, pieces[index], zone)
        zones.append(zone)
    zones = jnp.concatenate(zones, axis=1)
    patch_refs = upper_patches, lower_patches
    fill_patches(zones, half, side, patch_refs, slice(0, members * LANES))
    parts = products((upper_ref, lower_ref), patch_refs)
    sums = [jnp.zeros((out_rows, LANES), jnp.float32) for _ in range(3)]
    for member in range(members):
        for kernel in range(kernel_total):
            lanes = slice(member * LANES, (member + 1) * LANES)
            own = response_of(parts, kernel, kernel_total, lanes)
            place = 3 * (member * kernel_total + kernel)
            for order in range(3):
                sums[order] = sums[order] + factor_ref[place + order] * own
    lane = lax.broadcasted_iota(jnp.int32, (out_rows, LANES), 1)
    column = wide * tile_cols + jnp.where(lane < 2 * rim, lane - rim, tile_cols - 3 * rim + lane)
    x_coord = column_position(column, band_cols)
    border = sums[0] + x_coord * (sums[1] + x_coord * sums[2])
    border = jnp.where((column >= 0) & (column < band_cols), border, 0.0)

    middle = LANES // 2
    first_inner = inner_ref[:, :LANES]
    last_inner = inner_ref[:, tile_cols - LANES :]
    edge = jnp.where(
        lane < middle,
        jnp.where(lane < rim + half, border, pltpu.roll(first_inner, rim, 1)),
        jnp.where(
            lane >= LANES - rim - half,
            pltpu.roll(border, LANES - 4 * rim, 1),
            pltpu.roll(last_inner, LANES - rim, 1),
        ),
    )
    tall[...] = edge
    coadd_ref[...] = inner_ref[half : half + tile_rows, :]
    edge_detection = filtered(taps_ref, None, side, tall, tile_rows)
    edge_coadd = tall[half : half + tile_rows, :]
    detection_ref[...] = inner_detection_ref[...]
    lane = lane[:tile_rows]
    for out_ref, values, reach in (
        (coadd_ref, edge_coadd, half),
        (detection_ref, edge_detection, rim),
    ):
        head = pltpu.roll(values, LANES - rim, 1)
        tail = pltpu.roll(values, rim, 1)
        out_ref[:, :LANES] = jnp.where(lane < reach, head, out_ref[:, :LANES])
        out_ref[:, tile_cols - LANES :] = jnp.where(
            lane >= LANES - reach, tail, out_ref[:, tile_cols - LANES :]
        )


def on_device(
    exposures, basis_kernels, poly_coef, exposure_weight, row_start, row_count, filter_taps
):
    members, tile_rows, tile_cols = exposures.shape
    side = basis_kernels.shape[1]
    half, out_rows, in_rows = sizes(tile_rows, side)
    peers, wide_peers = lax.axis_size("narrow"), lax.axis_size("wide")
    vmem = pl.BlockSpec(memory_space=pltpu.VMEM)
    params = pltpu.CompilerParams(vmem_limit_bytes=VMEM_BYTES)

    def skipped(index):
        return 0 if any(abs(i - (i ^ index)) <= 1 for i in range(peers)) else 1

    sent = [skipped(index) for index in range(peers)]
    tiles = [exposures] * peers
    for index in reversed(range(1, peers)):
        pairs = [(i, i ^ index) for i in range(peers)]
        tiles[index] = lax.ppermute(exposures[sent[index] :], "narrow", pairs)
    taps, span, tables = prepared(
        basis_kernels,
        poly_coef,
        exposure_weight,
        row_start,
        row_count,
        filter_taps,
        tile_rows,
    )
    depth = side * PART
    edge_shape = jax.ShapeDtypeStruct((in_rows, LANES), exposures.dtype)
    window_shape = jax.ShapeDtypeStruct((members, in_rows, tile_cols), exposures.dtype)
    window, to_core, to_cross = pl.pallas_call(
        functools.partial(place_kernel, sent),
        out_shape=(window_shape, edge_shape, edge_shape),
        in_specs=[vmem] * (1 + peers),
        out_specs=[vmem] * 3,
        compiler_params=params,
        name="place",
    )(span, *reversed(tiles))
    core_pairs = [(i, i ^ 1) for i in range(wide_peers)]
    cross_pairs = []
    for row in range(peers):
        for column in range(wide_peers):
            other = ((column - 1) ^ 1) + 1
            if other in (-1, wide_peers):
                pair = (row ^ 1, column)
            else:
                pair = (row, other)
            cross_pairs.append((column * peers + row, pair[1] * peers + pair[0]))
    from_core = lax.ppermute(to_core, "wide", core_pairs)
    from_cross = lax.ppermute(to_cross, ("wide", "narrow"), cross_pairs)

    inner, inner_detection = pl.pallas_call(
        functools.partial(main_kernel, wide_peers, side, tile_rows),
        out_shape=(
            jax.ShapeDtypeStruct((out_rows, tile_cols), jnp.float32),
            jax.ShapeDtypeStruct((tile_rows, tile_cols), jnp.float32),
        ),
        in_specs=[vmem] * 6,
        out_specs=(vmem, vmem),
        scratch_shapes=[pltpu.VMEM((members // 2, depth, 2 * tile_cols), jnp.bfloat16)] * 2,
        compiler_params=params,
        cost_estimate=pl.CostEstimate(flops=2 * 10**9, bytes_accessed=10**6, transcendentals=0),
        name="main",
    )(*taps, *tables, window)
    out = jax.ShapeDtypeStruct((tile_rows, tile_cols), jnp.float32)
    return pl.pallas_call(
        functools.partial(rim_kernel, wide_peers, side, members),
        out_shape=(out, out),
        in_specs=[vmem] * 10,
        out_specs=(vmem, vmem),
        scratch_shapes=[
            pltpu.VMEM((depth, members * LANES), jnp.bfloat16),
            pltpu.VMEM((depth, members * LANES), jnp.bfloat16),
            pltpu.VMEM((out_rows, LANES), jnp.float32),
        ],
        compiler_params=params,
        name="rim",
    )(taps[0], *tables, inner, inner_detection, to_core, to_cross, from_core, from_cross)


def solution(mesh):
    placed = (P(None, "narrow", "wide"), P(), P(), P(), P(), P(), P())
    return jax.shard_map(
        on_device,
        mesh=mesh,
        in_specs=placed,
        out_specs=(P("narrow", "wide"), P("narrow", "wide")),
        check_vma=False,
    )
```

```python
import functools

import jax
import jax.numpy as jnp
from jax import lax
from jax.experimental import pallas as pl
from jax.experimental.pallas import tpu as pltpu
from jax.sharding import PartitionSpec as P

LANES = 128
VMEM_BYTES = 48 << 20


def rounded(value, unit):
    return -(-value // unit) * unit


def sizes(tile_rows, side):
    half = side // 2
    out_rows = rounded(tile_rows + 2 * half, 8)
    in_rows = rounded(tile_rows + 4 * half, 16)
    return half, out_rows, in_rows


UPPER = 24
PART = 48


def band_matrix(half, begin, base, band_ref):
    kernel_total, wide = len(base), base[0].shape[1]
    rows, depth = band_ref.shape
    place = lax.rem(lax.broadcasted_iota(jnp.int32, (8, wide), 1), PART)
    lead = begin - 2 * half
    parts = []
    for kernel in range(kernel_total):
        spread = jnp.broadcast_to(base[kernel], (8, wide))
        block = pltpu.roll(spread, 0, 1, stride=1, stride_axis=0)
        for first in range(0, rows // kernel_total, 8):
            shift = first + lead
            plain = pltpu.roll(block, shift % wide, 1)
            wrapped = pltpu.roll(block, (shift + (PART if lead < 0 else -PART)) % wide, 1)
            if lead < 0:
                parts.append(jnp.where(place < PART + lead - 4, plain, wrapped))
            else:
                parts.append(jnp.where(place < lead, wrapped, plain))
    band_ref[...] = jnp.concatenate(parts, axis=0).astype(jnp.bfloat16)[:, :depth]


def factors_kernel(
    tile_rows,
    band_rows,
    half,
    coef_ref,
    weight_ref,
    start_ref,
    count_ref,
    taps_ref,
    after_ref,
    factor_ref,
    spread_ref,
    span_ref,
):
    for tap in range(taps_ref.shape[0]):
        spread_ref[tap : tap + 1, :] = jnp.full((1, LANES), taps_ref[tap], jnp.float32)
    for member in range(start_ref.shape[0]):
        span_ref[member] = jnp.full((16, LANES), start_ref[member], jnp.int32)
        span_ref[start_ref.shape[0] + member] = jnp.full((16, LANES), count_ref[member], jnp.int32)

    kernel_total, members = coef_ref.shape[:2]
    out_rows = factor_ref.shape[1]
    place = lax.broadcasted_iota(jnp.int32, (out_rows, LANES), 0)
    row = lax.axis_index("narrow") * tile_rows - half + place
    y_coord = (2 * row + 1).astype(jnp.float32) / band_rows - 1.0
    weighting = []
    for member in range(members):
        inside = (row >= start_ref[member]) & (row < start_ref[member] + count_ref[member])
        weighting.append(jnp.where(inside, weight_ref[member], 0.0))
    denominator = functools.reduce(jnp.add, weighting)
    valid = (row >= 0) & (row < band_rows)
    inverse = jnp.where(valid, 1.0 / jnp.where(valid, denominator, 1.0), 0.0)
    for member in range(members):
        scale = weighting[member] * inverse
        for kernel in range(kernel_total):
            coeffs = [coef_ref[kernel, member, order] for order in range(6)]
            constant = coeffs[0] + coeffs[2] * y_coord + coeffs[5] * (y_coord * y_coord)
            index = 3 * (member * kernel_total + kernel)
            factor_ref[index] = constant * scale
            factor_ref[index + 1] = (coeffs[1] + coeffs[4] * y_coord) * scale
            factor_ref[index + 2] = coeffs[3] * scale


def spread_taps(basis_ref, square):
    kernel_total, side = basis_ref.shape[:2]
    rows = square.shape[0] // kernel_total
    wide = rounded(side * PART, LANES)
    square[...] = jnp.zeros_like(square)
    for kernel in range(kernel_total):
        square[kernel * rows : kernel * rows + side, :side] = basis_ref[kernel].astype(jnp.float32)
    across = lax.broadcasted_iota(jnp.int32, (LANES, wide), 0)
    begin = across * PART
    lane = lax.broadcasted_iota(jnp.int32, (LANES, wide), 1)
    onehot = jnp.where((lane >= begin) & (lane < begin + PART), 1.0, 0.0).astype(jnp.bfloat16)
    repeated = jnp.dot(
        square[...].astype(jnp.bfloat16), onehot, preferred_element_type=jnp.float32
    )
    down = lax.broadcasted_iota(jnp.int32, (rows, wide), 0)
    chosen = lax.rem(lax.broadcasted_iota(jnp.int32, (rows, wide), 1), PART) == down
    return [
        jnp.sum(
            jnp.where(chosen, repeated[kernel * rows : (kernel + 1) * rows], 0.0),
            axis=0,
            keepdims=True,
        )
        for kernel in range(kernel_total)
    ]


def bands_kernel(half, basis_ref, upper_ref, lower_ref, square):
    base = spread_taps(basis_ref, square)
    band_matrix(half, 0, base, upper_ref)
    band_matrix(half, UPPER, base, lower_ref)


def prepared(basis_kernels, poly_coef, weight, start, count, taps, tile_rows):
    kernel_total, side = basis_kernels.shape[:2]
    members = poly_coef.shape[0]
    half, out_rows, _ = sizes(tile_rows, side)
    depth = side * PART
    smem = pl.BlockSpec(memory_space=pltpu.SMEM)
    vmem = pl.BlockSpec(memory_space=pltpu.VMEM)
    params = pltpu.CompilerParams(vmem_limit_bytes=VMEM_BYTES)
    band_rows = lax.axis_size("narrow") * tile_rows
    upper, lower = pl.pallas_call(
        functools.partial(bands_kernel, half),
        out_shape=(
            jax.ShapeDtypeStruct((kernel_total * UPPER, depth), jnp.bfloat16),
            jax.ShapeDtypeStruct((kernel_total * (out_rows - UPPER), depth), jnp.bfloat16),
        ),
        in_specs=[vmem],
        out_specs=(vmem, vmem),
        scratch_shapes=[pltpu.VMEM((kernel_total * rounded(side, 8), LANES), jnp.float32)],
        compiler_params=params,
        cost_estimate=pl.CostEstimate(flops=10**9, bytes_accessed=10**6, transcendentals=0),
        name="bands",
    )(basis_kernels)
    factors, spread, span = pl.pallas_call(
        functools.partial(factors_kernel, tile_rows, band_rows, half),
        out_shape=(
            jax.ShapeDtypeStruct((3 * members * kernel_total, out_rows, LANES), jnp.float32),
            jax.ShapeDtypeStruct((side, LANES), jnp.float32),
            jax.ShapeDtypeStruct((2 * members, 16, LANES), jnp.int32),
        ),
        in_specs=[smem] * 5 + [pl.BlockSpec(memory_space=pl.ANY)],
        out_specs=(vmem, vmem, vmem),
        compiler_params=params,
        cost_estimate=pl.CostEstimate(flops=10**8, bytes_accessed=10**6, transcendentals=0),
        name="factors",
    )(poly_coef.transpose(1, 0, 2), weight, start, count, taps, upper)
    return spread, span, (factors, upper, lower)


def part_rows_of(moved):
    first, second, below, mixed, above = [moved[row : row + 16] for row in range(0, 80, 16)]
    place = lax.broadcasted_iota(jnp.int32, first.shape, 0)
    return (
        (first, jnp.where(place < 8, second, mixed), above),
        (jnp.where(place < 4, mixed, first), second, below),
    )


def fill_patches(window, half, side, patch_refs, lanes):
    width = window.shape[1]
    for tap in range(side):
        moved = pltpu.roll(window, (half - tap) % width, 1)
        for patch_ref, rows in zip(patch_refs, part_rows_of(moved), strict=True):
            for index, piece in enumerate(rows):
                begin = tap * PART + 16 * index
                patch_ref[begin : begin + 16, lanes] = piece


def products(band_refs, patch_refs):
    results = []
    for band_ref, patch_ref in zip(band_refs, patch_refs, strict=True):
        depth = band_ref.shape[1]
        pieces = []
        for begin in range(0, depth, 256):
            end = min(begin + 256, depth)
            pieces.append(
                jnp.dot(
                    band_ref[:, begin:end],
                    patch_ref[begin:end, :],
                    preferred_element_type=jnp.float32,
                )
            )
        results.append(functools.reduce(jnp.add, pieces))
    return results


def response_of(parts, kernel, kernel_total, lanes):
    pieces = []
    for part in parts:
        rows = part.shape[0] // kernel_total
        pieces.append(part[kernel * rows : (kernel + 1) * rows, lanes])
    return jnp.concatenate(pieces, axis=0)


def place_kernel(sent, span_ref, *refs):
    peers = len(sent)
    tiles = refs[:peers][::-1]
    window_ref, core_ref, cross_ref = refs[peers:]
    members, window_rows, tile_cols = window_ref.shape
    tile_rows = tiles[0].shape[1]
    narrow = lax.axis_index("narrow")
    odd = lax.rem(lax.axis_index("wide"), 2) == 1
    lane = lax.broadcasted_iota(jnp.int32, (window_rows, LANES), 1)
    place = lax.broadcasted_iota(jnp.int32, (16, tile_cols), 0)
    leftward = jnp.zeros((window_rows, LANES), jnp.bfloat16)
    rightward = jnp.zeros((window_rows, LANES), jnp.bfloat16)
    none = jnp.zeros((16, tile_cols), jnp.bfloat16)

    def over_columns(array):
        return jnp.concatenate([array] * (tile_cols // LANES), axis=1)

    for member in range(members):
        lead = over_columns(narrow * tile_rows - span_ref[member])
        count = over_columns(span_ref[members + member])
        here, below, above = [none] * 2, [none] * 2, [none] * 2
        for index in range(peers):
            if member < sent[index]:
                continue
            tile = [tiles[index][member - sent[index], row : row + 16] for row in (0, 16)]
            base = jnp.bitwise_xor(narrow, index) * tile_rows
            for parts, offset in ((here, 0), (below, tile_rows), (above, -tile_rows)):
                chosen = lead + offset == base
                for part in range(2):
                    parts[part] = jnp.where(chosen, tile[part], parts[part])
        upper = place < 8
        groups = (
            (here[0], place),
            (here[1], place + 16),
            (below[0], place + tile_rows),
            (
                jnp.where(upper, below[1], above[0]),
                place + jnp.where(upper, tile_rows + 16, -tile_rows),
            ),
            (above[1], place - 16),
        )
        kept = []
        for values, offset in groups:
            frame_row = lead + offset
            kept.append(jnp.where((frame_row >= 0) & (frame_row < count), values, none))
        window = jnp.concatenate(kept, axis=0)
        window_ref[member] = window
        own = lane // 32 == member
        first = pltpu.roll(window[:, :LANES], 32 * member, 1)
        last = pltpu.roll(window[:, tile_cols - LANES :], (32 * member + 32) % LANES, 1)
        leftward = jnp.where(own, first, leftward)
        rightward = jnp.where(own, last, rightward)

    @pl.when(odd)
    def _():
        core_ref[...] = leftward
        cross_ref[...] = rightward

    @pl.when(jnp.logical_not(odd))
    def _():
        core_ref[...] = rightward
        cross_ref[...] = leftward


def column_position(column, band_cols):
    return (2 * column + 1).astype(jnp.float32) / band_cols - 1.0


def filtered(taps_ref, side, tall, tile_rows):
    half = side // 2
    width = tall.shape[1]
    taps = [
        jnp.broadcast_to(
            jnp.concatenate([taps_ref[tap : tap + 1, :]] * (width // LANES), axis=1),
            (tile_rows, width),
        )
        for tap in range(side)
    ]
    across = taps[0] * tall[:tile_rows, :]
    for tap in range(1, side):
        across = across + taps[tap] * tall[tap : tap + tile_rows, :]
    result = taps[0] * pltpu.roll(across, half, 1)
    for tap in range(1, side):
        result = result + taps[tap] * pltpu.roll(across, (half - tap) % width, 1)
    return result


def main_kernel(
    wide_peers,
    side,
    tile_rows,
    taps_ref,
    factor_ref,
    upper_ref,
    lower_ref,
    window_ref,
    out_ref,
    inner_detection_ref,
    upper_patches,
    lower_patches,
):
    members, in_rows, tile_cols = window_ref.shape
    half, out_rows, _ = sizes(tile_rows, side)
    kernel_total = upper_ref.shape[0] // UPPER
    sums = [jnp.zeros((out_rows, tile_cols), jnp.float32) for _ in range(3)]
    group = upper_patches.shape[2] // tile_cols
    for begin in range(0, members, group):
        patch_refs = upper_patches.at[begin // group], lower_patches.at[begin // group]
        strips = [slice(index * tile_cols, (index + 1) * tile_cols) for index in range(group)]
        for index, lanes in enumerate(strips):
            fill_patches(window_ref[begin + index], half, side, patch_refs, lanes)
        parts = products((upper_ref, lower_ref), patch_refs)
        for index, lanes in enumerate(strips):
            for kernel in range(kernel_total):
                own = response_of(parts, kernel, kernel_total, lanes)
                place = 3 * ((begin + index) * kernel_total + kernel)
                for order in range(3):
                    factor = [factor_ref[place + order]] * (tile_cols // LANES)
                    sums[order] = sums[order] + jnp.concatenate(factor, axis=1) * own
    column = lax.axis_index("wide") * tile_cols + lax.broadcasted_iota(
        jnp.int32, (8, tile_cols), 1
    )
    x_coord = column_position(column, wide_peers * tile_cols)[:1]
    out_ref[...] = sums[0] + x_coord * (sums[1] + x_coord * sums[2])
    inner_detection_ref[...] = filtered(taps_ref, side, out_ref, tile_rows)


def rim_kernel(
    wide_peers,
    side,
    members,
    taps_ref,
    factor_ref,
    upper_ref,
    lower_ref,
    inner_ref,
    inner_detection_ref,
    to_core_ref,
    to_cross_ref,
    from_core_ref,
    from_cross_ref,
    coadd_ref,
    detection_ref,
    upper_patches,
    lower_patches,
    tall,
):
    tile_rows, tile_cols = coadd_ref.shape
    in_rows = to_core_ref.shape[0]
    half, out_rows, _ = sizes(tile_rows, side)
    rim = 2 * half
    kernel_total = upper_ref.shape[0] // UPPER
    band_cols = wide_peers * tile_cols
    wide = lax.axis_index("wide")
    odd = lax.rem(wide, 2) == 1

    none = jnp.zeros((in_rows, LANES), jnp.bfloat16)
    core, cross = from_core_ref[...], from_cross_ref[...]
    before = jnp.where(wide > 0, jnp.where(odd, core, cross), none)
    after = jnp.where(wide < wide_peers - 1, jnp.where(odd, cross, core), none)
    first = jnp.where(odd, to_core_ref[...], to_cross_ref[...])
    last = jnp.where(odd, to_cross_ref[...], to_core_ref[...])
    lane = lax.broadcasted_iota(jnp.int32, (in_rows, LANES), 1)
    zones = []
    for member in range(members):
        pieces = [
            pltpu.roll(piece, (target - 32 * member) % LANES, 1)
            for piece, target in ((before, -12), (first, rim), (last, 2 * rim - 12), (after, 3 * rim))
        ]
        zone = none
        for index in reversed(range(4)):
            zone = jnp.where(lane < (index + 1) * rim, pieces[index], zone)
        zones.append(zone)
    zones = jnp.concatenate(zones, axis=1)
    patch_refs = upper_patches, lower_patches
    fill_patches(zones, half, side, patch_refs, slice(0, members * LANES))
    parts = products((upper_ref, lower_ref), patch_refs)
    sums = [jnp.zeros((out_rows, LANES), jnp.float32) for _ in range(3)]
    for member in range(members):
        for kernel in range(kernel_total):
            lanes = slice(member * LANES, (member + 1) * LANES)
            own = response_of(parts, kernel, kernel_total, lanes)
            place = 3 * (member * kernel_total + kernel)
            for order in range(3):
                sums[order] = sums[order] + factor_ref[place + order] * own
    lane = lax.broadcasted_iota(jnp.int32, (out_rows, LANES), 1)
    column = wide * tile_cols + jnp.where(lane < 2 * rim, lane - rim, tile_cols - 3 * rim + lane)
    x_coord = column_position(column, band_cols)
    border = sums[0] + x_coord * (sums[1] + x_coord * sums[2])
    border = jnp.where((column >= 0) & (column < band_cols), border, 0.0)

    middle = LANES // 2
    first_inner = inner_ref[:, :LANES]
    last_inner = inner_ref[:, tile_cols - LANES :]
    edge = jnp.where(
        lane < middle,
        jnp.where(lane < rim + half, border, pltpu.roll(first_inner, rim, 1)),
        jnp.where(
            lane >= LANES - rim - half,
            pltpu.roll(border, LANES - 4 * rim, 1),
            pltpu.roll(last_inner, LANES - rim, 1),
        ),
    )
    tall[...] = edge
    edge_detection = filtered(taps_ref, side, tall, tile_rows)
    edge_coadd = tall[half : half + tile_rows, :]
    lane = lane[:tile_rows]
    for out_ref, inner, values, reach in (
        (coadd_ref, inner_ref[half : half + tile_rows, :], edge_coadd, half),
        (detection_ref, inner_detection_ref[...], edge_detection, rim),
    ):
        head = pltpu.roll(values, LANES - rim, 1)
        tail = pltpu.roll(values, rim, 1)
        last = tile_cols - LANES
        out_ref[:, :LANES] = jnp.where(lane < reach, head, inner[:, :LANES])
        out_ref[:, LANES:last] = inner[:, LANES:last]
        out_ref[:, last:] = jnp.where(lane >= LANES - reach, tail, inner[:, last:])


def on_device(
    exposures, basis_kernels, poly_coef, exposure_weight, row_start, row_count, filter_taps
):
    members, tile_rows, tile_cols = exposures.shape
    side = basis_kernels.shape[1]
    half, out_rows, in_rows = sizes(tile_rows, side)
    peers, wide_peers = lax.axis_size("narrow"), lax.axis_size("wide")
    vmem = pl.BlockSpec(memory_space=pltpu.VMEM)
    params = pltpu.CompilerParams(vmem_limit_bytes=VMEM_BYTES)

    def skipped(index):
        return 0 if any(abs(i - (i ^ index)) <= 1 for i in range(peers)) else 1

    sent = [skipped(index) for index in range(peers)]
    tiles = [exposures] * peers
    for index in reversed(range(1, peers)):
        pairs = [(i, i ^ index) for i in range(peers)]
        tiles[index] = lax.ppermute(exposures[sent[index] :], "narrow", pairs)
    taps, span, tables = prepared(
        basis_kernels,
        poly_coef,
        exposure_weight,
        row_start,
        row_count,
        filter_taps,
        tile_rows,
    )
    depth = side * PART
    edge_shape = jax.ShapeDtypeStruct((in_rows, LANES), exposures.dtype)
    window_shape = jax.ShapeDtypeStruct((members, in_rows, tile_cols), exposures.dtype)
    window, to_core, to_cross = pl.pallas_call(
        functools.partial(place_kernel, sent),
        out_shape=(window_shape, edge_shape, edge_shape),
        in_specs=[vmem] * (1 + peers),
        out_specs=[vmem] * 3,
        compiler_params=params,
        name="place",
    )(span, *reversed(tiles))
    core_pairs = [(i, i ^ 1) for i in range(wide_peers)]
    cross_pairs = []
    for row in range(peers):
        for column in range(wide_peers):
            other = ((column - 1) ^ 1) + 1
            if other in (-1, wide_peers):
                pair = (row ^ 1, column)
            else:
                pair = (row, other)
            cross_pairs.append((column * peers + row, pair[1] * peers + pair[0]))
    from_core = lax.ppermute(to_core, "wide", core_pairs)
    from_cross = lax.ppermute(to_cross, ("wide", "narrow"), cross_pairs)

    inner, inner_detection = pl.pallas_call(
        functools.partial(main_kernel, wide_peers, side, tile_rows),
        out_shape=(
            jax.ShapeDtypeStruct((out_rows, tile_cols), jnp.float32),
            jax.ShapeDtypeStruct((tile_rows, tile_cols), jnp.float32),
        ),
        in_specs=[vmem] * 5,
        out_specs=(vmem, vmem),
        scratch_shapes=[pltpu.VMEM((members // 2, depth, 2 * tile_cols), jnp.bfloat16)] * 2,
        compiler_params=params,
        cost_estimate=pl.CostEstimate(flops=2 * 10**9, bytes_accessed=10**6, transcendentals=0),
        name="main",
    )(taps, *tables, window)
    out = jax.ShapeDtypeStruct((tile_rows, tile_cols), jnp.float32)
    return pl.pallas_call(
        functools.partial(rim_kernel, wide_peers, side, members),
        out_shape=(out, out),
        in_specs=[vmem] * 10,
        out_specs=(vmem, vmem),
        scratch_shapes=[
            pltpu.VMEM((depth, members * LANES), jnp.bfloat16),
            pltpu.VMEM((depth, members * LANES), jnp.bfloat16),
            pltpu.VMEM((out_rows, LANES), jnp.float32),
        ],
        compiler_params=params,
        name="rim",
    )(taps, *tables, inner, inner_detection, to_core, to_cross, from_core, from_cross)


def solution(mesh):
    placed = (P(None, "narrow", "wide"), P(), P(), P(), P(), P(), P())
    return jax.shard_map(
        on_device,
        mesh=mesh,
        in_specs=placed,
        out_specs=(P("narrow", "wide"), P("narrow", "wide")),
        check_vma=False,
    )
```

```python
import functools

import jax
import jax.numpy as jnp
from jax import lax
from jax.experimental import pallas as pl
from jax.experimental.pallas import tpu as pltpu
from jax.sharding import PartitionSpec as P

LANES = 128
VMEM_BYTES = 48 << 20


def rounded(value, unit):
    return -(-value // unit) * unit


def sizes(tile_rows, side):
    half = side // 2
    out_rows = rounded(tile_rows + 2 * half, 8)
    in_rows = rounded(tile_rows + 4 * half, 16)
    return half, out_rows, in_rows


UPPER = 24
PART = 48


def band_matrix(half, begin, base, band_ref):
    kernel_total, wide = len(base), base[0].shape[1]
    rows, depth = band_ref.shape
    place = lax.rem(lax.broadcasted_iota(jnp.int32, (8, wide), 1), PART)
    lead = begin - 2 * half
    parts = []
    for kernel in range(kernel_total):
        spread = jnp.broadcast_to(base[kernel], (8, wide))
        block = pltpu.roll(spread, 0, 1, stride=1, stride_axis=0)
        for first in range(0, rows // kernel_total, 8):
            shift = first + lead
            plain = pltpu.roll(block, shift % wide, 1)
            wrapped = pltpu.roll(block, (shift + (PART if lead < 0 else -PART)) % wide, 1)
            if lead < 0:
                parts.append(jnp.where(place < PART + lead - 4, plain, wrapped))
            else:
                parts.append(jnp.where(place < lead, wrapped, plain))
    band_ref[...] = jnp.concatenate(parts, axis=0).astype(jnp.bfloat16)[:, :depth]


def factors_kernel(
    tile_rows,
    band_rows,
    half,
    coef_ref,
    weight_ref,
    start_ref,
    count_ref,
    taps_ref,
    after_ref,
    factor_ref,
    spread_ref,
    span_ref,
    rows_ref,
):
    wide = lax.broadcasted_iota(jnp.int32, (8, LANES), 1)
    line = jnp.zeros((8, LANES), jnp.float32)
    for tap in range(taps_ref.shape[0]):
        line = jnp.where(wide == tap, taps_ref[tap], line)
    tile = pltpu.roll(line, 0, 1, stride=1, stride_axis=0)
    grid = [pltpu.roll(tile, first, 1) for first in range(0, rows_ref.shape[0] // 2, 8)]
    grid = jnp.concatenate(grid, axis=0)
    high = grid.astype(jnp.bfloat16).astype(jnp.float32)
    both = high + pltpu.roll(high, LANES // 2, 1)
    rows_ref[...] = jnp.concatenate([both, grid - high], axis=0).astype(jnp.bfloat16)
    for tap in range(taps_ref.shape[0]):
        spread_ref[tap : tap + 1, :] = jnp.full((1, LANES), taps_ref[tap], jnp.float32)
    for member in range(start_ref.shape[0]):
        span_ref[member] = jnp.full((16, LANES), start_ref[member], jnp.int32)
        span_ref[start_ref.shape[0] + member] = jnp.full((16, LANES), count_ref[member], jnp.int32)

    kernel_total, members = coef_ref.shape[:2]
    out_rows = factor_ref.shape[1]
    place = lax.broadcasted_iota(jnp.int32, (out_rows, LANES), 0)
    row = lax.axis_index("narrow") * tile_rows - half + place
    y_coord = (2 * row + 1).astype(jnp.float32) / band_rows - 1.0
    weighting = []
    for member in range(members):
        inside = (row >= start_ref[member]) & (row < start_ref[member] + count_ref[member])
        weighting.append(jnp.where(inside, weight_ref[member], 0.0))
    denominator = functools.reduce(jnp.add, weighting)
    valid = (row >= 0) & (row < band_rows)
    inverse = jnp.where(valid, 1.0 / jnp.where(valid, denominator, 1.0), 0.0)
    for member in range(members):
        scale = weighting[member] * inverse
        for kernel in range(kernel_total):
            coeffs = [coef_ref[kernel, member, order] for order in range(6)]
            constant = coeffs[0] + coeffs[2] * y_coord + coeffs[5] * (y_coord * y_coord)
            index = 3 * (member * kernel_total + kernel)
            factor_ref[index] = constant * scale
            factor_ref[index + 1] = (coeffs[1] + coeffs[4] * y_coord) * scale
            factor_ref[index + 2] = coeffs[3] * scale


def spread_taps(basis_ref, square):
    kernel_total, side = basis_ref.shape[:2]
    rows = square.shape[0] // kernel_total
    wide = rounded(side * PART, LANES)
    square[...] = jnp.zeros_like(square)
    for kernel in range(kernel_total):
        square[kernel * rows : kernel * rows + side, :side] = basis_ref[kernel].astype(jnp.float32)
    across = lax.broadcasted_iota(jnp.int32, (LANES, wide), 0)
    begin = across * PART
    lane = lax.broadcasted_iota(jnp.int32, (LANES, wide), 1)
    onehot = jnp.where((lane >= begin) & (lane < begin + PART), 1.0, 0.0).astype(jnp.bfloat16)
    repeated = jnp.dot(
        square[...].astype(jnp.bfloat16), onehot, preferred_element_type=jnp.float32
    )
    down = lax.broadcasted_iota(jnp.int32, (rows, wide), 0)
    chosen = lax.rem(lax.broadcasted_iota(jnp.int32, (rows, wide), 1), PART) == down
    return [
        jnp.sum(
            jnp.where(chosen, repeated[kernel * rows : (kernel + 1) * rows], 0.0),
            axis=0,
            keepdims=True,
        )
        for kernel in range(kernel_total)
    ]


def bands_kernel(half, basis_ref, upper_ref, lower_ref, square):
    base = spread_taps(basis_ref, square)
    band_matrix(half, 0, base, upper_ref)
    band_matrix(half, UPPER, base, lower_ref)


def prepared(basis_kernels, poly_coef, weight, start, count, taps, tile_rows):
    kernel_total, side = basis_kernels.shape[:2]
    members = poly_coef.shape[0]
    half, out_rows, _ = sizes(tile_rows, side)
    depth = side * PART
    smem = pl.BlockSpec(memory_space=pltpu.SMEM)
    vmem = pl.BlockSpec(memory_space=pltpu.VMEM)
    params = pltpu.CompilerParams(vmem_limit_bytes=VMEM_BYTES)
    band_rows = lax.axis_size("narrow") * tile_rows
    upper, lower = pl.pallas_call(
        functools.partial(bands_kernel, half),
        out_shape=(
            jax.ShapeDtypeStruct((kernel_total * UPPER, depth), jnp.bfloat16),
            jax.ShapeDtypeStruct((kernel_total * (out_rows - UPPER), depth), jnp.bfloat16),
        ),
        in_specs=[vmem],
        out_specs=(vmem, vmem),
        scratch_shapes=[pltpu.VMEM((kernel_total * rounded(side, 8), LANES), jnp.float32)],
        compiler_params=params,
        cost_estimate=pl.CostEstimate(flops=10**9, bytes_accessed=10**6, transcendentals=0),
        name="bands",
    )(basis_kernels)
    factors, spread, span, rows = pl.pallas_call(
        functools.partial(factors_kernel, tile_rows, band_rows, half),
        out_shape=(
            jax.ShapeDtypeStruct((3 * members * kernel_total, out_rows, LANES), jnp.float32),
            jax.ShapeDtypeStruct((side, LANES), jnp.float32),
            jax.ShapeDtypeStruct((2 * members, 16, LANES), jnp.int32),
            jax.ShapeDtypeStruct((2 * tile_rows, LANES), jnp.bfloat16),
        ),
        in_specs=[smem] * 5 + [pl.BlockSpec(memory_space=pl.ANY)],
        out_specs=(vmem, vmem, vmem, vmem),
        compiler_params=params,
        cost_estimate=pl.CostEstimate(flops=10**8, bytes_accessed=10**6, transcendentals=0),
        name="factors",
    )(poly_coef.transpose(1, 0, 2), weight, start, count, taps, upper)
    return (spread, rows), span, (factors, upper, lower)


def part_rows_of(moved):
    first, second, below, mixed, above = [moved[row : row + 16] for row in range(0, 80, 16)]
    place = lax.broadcasted_iota(jnp.int32, first.shape, 0)
    return (
        (first, jnp.where(place < 8, second, mixed), above),
        (jnp.where(place < 4, mixed, first), second, below),
    )


def fill_patches(window, half, side, patch_refs, lanes):
    width = window.shape[1]
    for tap in range(side):
        moved = pltpu.roll(window, (half - tap) % width, 1)
        for patch_ref, rows in zip(patch_refs, part_rows_of(moved), strict=True):
            for index, piece in enumerate(rows):
                begin = tap * PART + 16 * index
                patch_ref[begin : begin + 16, lanes] = piece


def products(band_refs, patch_refs):
    results = []
    for band_ref, patch_ref in zip(band_refs, patch_refs, strict=True):
        depth = band_ref.shape[1]
        pieces = []
        for begin in range(0, depth, 256):
            end = min(begin + 256, depth)
            pieces.append(
                jnp.dot(
                    band_ref[:, begin:end],
                    patch_ref[begin:end, :],
                    preferred_element_type=jnp.float32,
                )
            )
        results.append(functools.reduce(jnp.add, pieces))
    return results


def response_of(parts, kernel, kernel_total, lanes):
    pieces = []
    for part in parts:
        rows = part.shape[0] // kernel_total
        pieces.append(part[kernel * rows : (kernel + 1) * rows, lanes])
    return jnp.concatenate(pieces, axis=0)


def place_kernel(sent, span_ref, *refs):
    peers = len(sent)
    tiles = refs[:peers][::-1]
    window_ref, core_ref, cross_ref = refs[peers:]
    members, window_rows, tile_cols = window_ref.shape
    tile_rows = tiles[0].shape[1]
    narrow = lax.axis_index("narrow")
    odd = lax.rem(lax.axis_index("wide"), 2) == 1
    lane = lax.broadcasted_iota(jnp.int32, (window_rows, LANES), 1)
    place = lax.broadcasted_iota(jnp.int32, (16, tile_cols), 0)
    leftward = jnp.zeros((window_rows, LANES), jnp.bfloat16)
    rightward = jnp.zeros((window_rows, LANES), jnp.bfloat16)
    none = jnp.zeros((16, tile_cols), jnp.bfloat16)

    def over_columns(array):
        return jnp.concatenate([array] * (tile_cols // LANES), axis=1)

    for member in range(members):
        lead = over_columns(narrow * tile_rows - span_ref[member])
        count = over_columns(span_ref[members + member])
        here, below, above = [none] * 2, [none] * 2, [none] * 2
        for index in range(peers):
            if member < sent[index]:
                continue
            tile = [tiles[index][member - sent[index], row : row + 16] for row in (0, 16)]
            base = jnp.bitwise_xor(narrow, index) * tile_rows
            for parts, offset in ((here, 0), (below, tile_rows), (above, -tile_rows)):
                chosen = lead + offset == base
                for part in range(2):
                    parts[part] = jnp.where(chosen, tile[part], parts[part])
        upper = place < 8
        groups = (
            (here[0], place),
            (here[1], place + 16),
            (below[0], place + tile_rows),
            (
                jnp.where(upper, below[1], above[0]),
                place + jnp.where(upper, tile_rows + 16, -tile_rows),
            ),
            (above[1], place - 16),
        )
        kept = []
        for values, offset in groups:
            frame_row = lead + offset
            kept.append(jnp.where((frame_row >= 0) & (frame_row < count), values, none))
        window = jnp.concatenate(kept, axis=0)
        window_ref[member] = window
        own = lane // 32 == member
        first = pltpu.roll(window[:, :LANES], 32 * member, 1)
        last = pltpu.roll(window[:, tile_cols - LANES :], (32 * member + 32) % LANES, 1)
        leftward = jnp.where(own, first, leftward)
        rightward = jnp.where(own, last, rightward)

    @pl.when(odd)
    def _():
        core_ref[...] = leftward
        cross_ref[...] = rightward

    @pl.when(jnp.logical_not(odd))
    def _():
        core_ref[...] = rightward
        cross_ref[...] = leftward


def column_position(column, band_cols):
    return (2 * column + 1).astype(jnp.float32) / band_cols - 1.0


def filtered(taps_ref, rows_ref, side, tall, tile_rows):
    half = side // 2
    width = tall.shape[1]
    taps = [
        jnp.broadcast_to(
            jnp.concatenate([taps_ref[tap : tap + 1, :]] * (width // LANES), axis=1),
            (tile_rows, width),
        )
        for tap in range(side)
    ]
    if rows_ref is None:
        across = taps[0] * tall[:tile_rows, :]
        for tap in range(1, side):
            across = across + taps[tap] * tall[tap : tap + tile_rows, :]
    else:
        coadded = jnp.concatenate(
            [tall, jnp.zeros((LANES // 2 - tall.shape[0], width), jnp.float32)], axis=0
        )
        high = coadded.astype(jnp.bfloat16)
        low = (coadded - high.astype(jnp.float32)).astype(jnp.bfloat16)
        split = jnp.concatenate([high, low], axis=0)
        across = jnp.dot(rows_ref[...], split, preferred_element_type=jnp.float32)
        across = across[:tile_rows] + across[tile_rows:]
    result = taps[0] * pltpu.roll(across, half, 1)
    for tap in range(1, side):
        result = result + taps[tap] * pltpu.roll(across, (half - tap) % width, 1)
    return result


def main_kernel(
    wide_peers,
    side,
    tile_rows,
    taps_ref,
    rows_ref,
    factor_ref,
    upper_ref,
    lower_ref,
    window_ref,
    out_ref,
    inner_detection_ref,
    upper_patches,
    lower_patches,
):
    members, in_rows, tile_cols = window_ref.shape
    half, out_rows, _ = sizes(tile_rows, side)
    kernel_total = upper_ref.shape[0] // UPPER
    sums = [jnp.zeros((out_rows, tile_cols), jnp.float32) for _ in range(3)]
    group = upper_patches.shape[2] // tile_cols
    for begin in range(0, members, group):
        patch_refs = upper_patches.at[begin // group], lower_patches.at[begin // group]
        strips = [slice(index * tile_cols, (index + 1) * tile_cols) for index in range(group)]
        for index, lanes in enumerate(strips):
            fill_patches(window_ref[begin + index], half, side, patch_refs, lanes)
        parts = products((upper_ref, lower_ref), patch_refs)
        for index, lanes in enumerate(strips):
            for kernel in range(kernel_total):
                own = response_of(parts, kernel, kernel_total, lanes)
                place = 3 * ((begin + index) * kernel_total + kernel)
                for order in range(3):
                    factor = [factor_ref[place + order]] * (tile_cols // LANES)
                    sums[order] = sums[order] + jnp.concatenate(factor, axis=1) * own
    column = lax.axis_index("wide") * tile_cols + lax.broadcasted_iota(
        jnp.int32, (8, tile_cols), 1
    )
    x_coord = column_position(column, wide_peers * tile_cols)[:1]
    coadded = sums[0] + x_coord * (sums[1] + x_coord * sums[2])
    out_ref[...] = coadded
    inner_detection_ref[...] = filtered(taps_ref, rows_ref, side, coadded, tile_rows)


def rim_kernel(
    wide_peers,
    side,
    members,
    taps_ref,
    factor_ref,
    upper_ref,
    lower_ref,
    inner_ref,
    inner_detection_ref,
    to_core_ref,
    to_cross_ref,
    from_core_ref,
    from_cross_ref,
    coadd_ref,
    detection_ref,
    upper_patches,
    lower_patches,
    tall,
):
    tile_rows, tile_cols = coadd_ref.shape
    in_rows = to_core_ref.shape[0]
    half, out_rows, _ = sizes(tile_rows, side)
    rim = 2 * half
    kernel_total = upper_ref.shape[0] // UPPER
    band_cols = wide_peers * tile_cols
    wide = lax.axis_index("wide")
    odd = lax.rem(wide, 2) == 1

    none = jnp.zeros((in_rows, LANES), jnp.bfloat16)
    core, cross = from_core_ref[...], from_cross_ref[...]
    before = jnp.where(wide > 0, jnp.where(odd, core, cross), none)
    after = jnp.where(wide < wide_peers - 1, jnp.where(odd, cross, core), none)
    first = jnp.where(odd, to_core_ref[...], to_cross_ref[...])
    last = jnp.where(odd, to_cross_ref[...], to_core_ref[...])
    lane = lax.broadcasted_iota(jnp.int32, (in_rows, LANES), 1)
    zones = []
    for member in range(members):
        pieces = [
            pltpu.roll(piece, (target - 32 * member) % LANES, 1)
            for piece, target in ((before, -12), (first, rim), (last, 2 * rim - 12), (after, 3 * rim))
        ]
        zone = none
        for index in reversed(range(4)):
            zone = jnp.where(lane < (index + 1) * rim, pieces[index], zone)
        zones.append(zone)
    zones = jnp.concatenate(zones, axis=1)
    patch_refs = upper_patches, lower_patches
    fill_patches(zones, half, side, patch_refs, slice(0, members * LANES))
    parts = products((upper_ref, lower_ref), patch_refs)
    sums = [jnp.zeros((out_rows, LANES), jnp.float32) for _ in range(3)]
    for member in range(members):
        for kernel in range(kernel_total):
            lanes = slice(member * LANES, (member + 1) * LANES)
            own = response_of(parts, kernel, kernel_total, lanes)
            place = 3 * (member * kernel_total + kernel)
            for order in range(3):
                sums[order] = sums[order] + factor_ref[place + order] * own
    lane = lax.broadcasted_iota(jnp.int32, (out_rows, LANES), 1)
    column = wide * tile_cols + jnp.where(lane < 2 * rim, lane - rim, tile_cols - 3 * rim + lane)
    x_coord = column_position(column, band_cols)
    border = sums[0] + x_coord * (sums[1] + x_coord * sums[2])
    border = jnp.where((column >= 0) & (column < band_cols), border, 0.0)

    middle = LANES // 2
    first_inner = inner_ref[:, :LANES]
    last_inner = inner_ref[:, tile_cols - LANES :]
    edge = jnp.where(
        lane < middle,
        jnp.where(lane < rim + half, border, pltpu.roll(first_inner, rim, 1)),
        jnp.where(
            lane >= LANES - rim - half,
            pltpu.roll(border, LANES - 4 * rim, 1),
            pltpu.roll(last_inner, LANES - rim, 1),
        ),
    )
    tall[...] = edge
    edge_detection = filtered(taps_ref, None, side, tall, tile_rows)
    edge_coadd = tall[half : half + tile_rows, :]
    lane = lane[:tile_rows]
    for out_ref, inner, values, reach in (
        (coadd_ref, inner_ref[half : half + tile_rows, :], edge_coadd, half),
        (detection_ref, inner_detection_ref[...], edge_detection, rim),
    ):
        head = pltpu.roll(values, LANES - rim, 1)
        tail = pltpu.roll(values, rim, 1)
        last = tile_cols - LANES
        out_ref[:, :LANES] = jnp.where(lane < reach, head, inner[:, :LANES])
        out_ref[:, LANES:last] = inner[:, LANES:last]
        out_ref[:, last:] = jnp.where(lane >= LANES - reach, tail, inner[:, last:])


def on_device(
    exposures, basis_kernels, poly_coef, exposure_weight, row_start, row_count, filter_taps
):
    members, tile_rows, tile_cols = exposures.shape
    side = basis_kernels.shape[1]
    half, out_rows, in_rows = sizes(tile_rows, side)
    peers, wide_peers = lax.axis_size("narrow"), lax.axis_size("wide")
    vmem = pl.BlockSpec(memory_space=pltpu.VMEM)
    params = pltpu.CompilerParams(vmem_limit_bytes=VMEM_BYTES)

    def skipped(index):
        return 0 if any(abs(i - (i ^ index)) <= 1 for i in range(peers)) else 1

    sent = [skipped(index) for index in range(peers)]
    tiles = [exposures] * peers
    for index in reversed(range(1, peers)):
        pairs = [(i, i ^ index) for i in range(peers)]
        tiles[index] = lax.ppermute(exposures[sent[index] :], "narrow", pairs)
    taps, span, tables = prepared(
        basis_kernels,
        poly_coef,
        exposure_weight,
        row_start,
        row_count,
        filter_taps,
        tile_rows,
    )
    depth = side * PART
    edge_shape = jax.ShapeDtypeStruct((in_rows, LANES), exposures.dtype)
    window_shape = jax.ShapeDtypeStruct((members, in_rows, tile_cols), exposures.dtype)
    window, to_core, to_cross = pl.pallas_call(
        functools.partial(place_kernel, sent),
        out_shape=(window_shape, edge_shape, edge_shape),
        in_specs=[vmem] * (1 + peers),
        out_specs=[vmem] * 3,
        compiler_params=params,
        name="place",
    )(span, *reversed(tiles))
    core_pairs = [(i, i ^ 1) for i in range(wide_peers)]
    cross_pairs = []
    for row in range(peers):
        for column in range(wide_peers):
            other = ((column - 1) ^ 1) + 1
            if other in (-1, wide_peers):
                pair = (row ^ 1, column)
            else:
                pair = (row, other)
            cross_pairs.append((column * peers + row, pair[1] * peers + pair[0]))
    from_core = lax.ppermute(to_core, "wide", core_pairs)
    from_cross = lax.ppermute(to_cross, ("wide", "narrow"), cross_pairs)

    inner, inner_detection = pl.pallas_call(
        functools.partial(main_kernel, wide_peers, side, tile_rows),
        out_shape=(
            jax.ShapeDtypeStruct((out_rows, tile_cols), jnp.float32),
            jax.ShapeDtypeStruct((tile_rows, tile_cols), jnp.float32),
        ),
        in_specs=[vmem] * 6,
        out_specs=(vmem, vmem),
        scratch_shapes=[pltpu.VMEM((members // 2, depth, 2 * tile_cols), jnp.bfloat16)] * 2,
        compiler_params=params,
        cost_estimate=pl.CostEstimate(flops=2 * 10**9, bytes_accessed=10**6, transcendentals=0),
        name="main",
    )(*taps, *tables, window)
    out = jax.ShapeDtypeStruct((tile_rows, tile_cols), jnp.float32)
    return pl.pallas_call(
        functools.partial(rim_kernel, wide_peers, side, members),
        out_shape=(out, out),
        in_specs=[vmem] * 10,
        out_specs=(vmem, vmem),
        scratch_shapes=[
            pltpu.VMEM((depth, members * LANES), jnp.bfloat16),
            pltpu.VMEM((depth, members * LANES), jnp.bfloat16),
            pltpu.VMEM((out_rows, LANES), jnp.float32),
        ],
        compiler_params=params,
        name="rim",
    )(taps[0], *tables, inner, inner_detection, to_core, to_cross, from_core, from_cross)


def solution(mesh):
    placed = (P(None, "narrow", "wide"), P(), P(), P(), P(), P(), P())
    return jax.shard_map(
        on_device,
        mesh=mesh,
        in_specs=placed,
        out_specs=(P("narrow", "wide"), P("narrow", "wide")),
        check_vma=False,
    )
```
